512 devices in a mesh: dp: 64 (over z_hi, y, core), mp: 8 (over x, z_lo).
Axes of the slice: x: 4, y: 8, z: 8 (z_hi: 4, z_lo: 2; z = z_hi * 2 + z_lo), core: 2. Of those that a mesh axis runs over, the one named last changes fastest.
Arguments:
- tokens: bfloat16 [9216, 4096], P('dp'), may hold values from -6 to 6
- cotangent: bfloat16 [9216, 4096], P('dp'), may hold values from -6 to 6
- gate_blocks: bfloat16 [64, 128, 128], P('dp'), may hold values from -0.5 to 0.5
- up_blocks: bfloat16 [64, 128, 128], P('dp'), may hold values from -0.5 to 0.5
- down_blocks: bfloat16 [64, 128, 128], P('dp'), may hold values from -0.5 to 0.5
- col_block: int32 [64], replicated, may hold values from 0 to 223, as said below
- in_row: int32 [64], replicated, may hold values from 0 to 31, as said below
- out_row: int32 [64], replicated, may hold values from 0 to 31
Outputs:
- input_grad: bfloat16 [9216, 4096], P('dp', 'mp')
- gate_grads: float32 [64, 128, 128], P('dp')
- up_grads: float32 [64, 128, 128], P('dp')
- down_grads: float32 [64, 128, 128], P('dp')
The draws below stay inside these ranges and needn't reach their ends.
Inputs may be any that keep to these rules, and one draw needn't show every extreme that they name: Flat blocks are ordered by owner: floor(col_block / 28) never falls along the list. Each owner holds 1 to 20 blocks, and some owner holds exactly 20. The pairs (in_row, col_block) are distinct, and so are the pairs (col_block, out_row). `in_row`: gate and up blocks share positions.
All inputs are finite; a program needn't handle non-finite values.
Results may differ from the reference program's by a relative error of at most 0.007.
Values may be sent and summed in bfloat16 or wider, within the bound.
A program may use at most 64 MiB of HBM per device.

```python
import jax
import jax.numpy as jnp
from jax import lax

BLK = 128
D = 4096
FF = 28672
TOK_DEV = 144
NB = 64
CAP = 20
TOKENS = 9216
N_MP = 8


def pattern_draw(key):
    base_key = jax.random.fold_in(key, 4242)
    key_busy, key_weight, key_order, key_slots, key_shift = jax.random.split(base_key, 5)
    owners = jnp.arange(N_MP, dtype=jnp.int32)
    busy_owner = jax.random.randint(key_busy, (), 0, N_MP)
    weights = jnp.where(owners == busy_owner, 0, jax.random.randint(key_weight, (N_MP,), 1, 5))
    spare_units = NB - CAP - (N_MP - 1)
    shares = spare_units * weights // jnp.sum(weights)
    leftover = spare_units - jnp.sum(shares)
    owner_order = jax.random.permutation(key_order, N_MP)
    position = jnp.zeros((N_MP,), jnp.int32).at[owner_order].set(owners)
    busy_pos = position[busy_owner]
    ranked = position - (position > busy_pos).astype(jnp.int32)
    extra_unit = ((ranked < leftover) & (owners != busy_owner)).astype(jnp.int32)
    counts = jnp.where(owners == busy_owner, CAP, 1 + shares + extra_unit)
    starts = jnp.cumsum(counts) - counts
    flat_ids = jnp.arange(NB, dtype=jnp.int32)
    owner_ids = jnp.sum((flat_ids[:, None] >= starts[None, 1:]).astype(jnp.int32), axis=1)
    local_ids = flat_ids - starts[owner_ids]
    owned_cols = FF // (BLK * N_MP)
    row_blocks = D // BLK

    def owner_slots(owner_key):
        return jax.random.permutation(owner_key, row_blocks * owned_cols)
    slot_table = jax.vmap(owner_slots)(jax.random.split(key_slots, N_MP))
    chosen = slot_table[owner_ids, local_ids]
    col_local = chosen % owned_cols
    row_ids = chosen // owned_cols
    shifts = jax.random.randint(key_shift, (N_MP, owned_cols), 0, row_blocks)
    out_ids = (row_ids + shifts[owner_ids, col_local]) % row_blocks
    return ((owner_ids * owned_cols + col_local).astype(jnp.int32), row_ids.astype(jnp.int32), out_ids.astype(jnp.int32))


def draw_col_block(key, part):
    return pattern_draw(key)[0]


def draw_in_row(key, part):
    return pattern_draw(key)[1]


def draw_out_row(key, part):
    return pattern_draw(key)[2]


def steps_of(key, shape, pieces, least, top_value):
    def one(dim, parts):
        heights = jax.random.uniform(jax.random.fold_in(jax.random.fold_in(key, 6), dim), (parts,), jnp.float32, least / len(pieces), top_value / len(pieces))
        return jnp.repeat(jnp.exp(heights), shape[dim] // parts).reshape((-1,) + (1,) * (len(shape) - dim - 1))

    level = one(*pieces[0])
    for cut in pieces[1:]:
        level = level * one(*cut)
    return level


def noise(rng, shape, width, most, cuts=(), kind=jnp.bfloat16):
    array = jax.random.normal(rng, shape, jnp.float32) * width
    if len(cuts) > 0:
        array = steps_of(rng, shape, cuts, -0.22, 0.18) * array
    return jnp.clip(array, min=-most, max=most).astype(kind)


def setup_inputs(seed: int = 0) -> dict:
    keys = jax.random.split(jax.random.key(seed), 9)
    return {
        "tokens": noise(keys[0], (TOKENS, D), 1.0, 6.0, ((0, 64),)),
        "cotangent": noise(keys[1], (TOKENS, D), 1.0, 6.0, ((0, 64),)),
        "gate_blocks": noise(keys[2], (NB, BLK, BLK), BLK ** -0.5, 0.5, ((0, 64),)),
        "up_blocks": noise(keys[3], (NB, BLK, BLK), BLK ** -0.5, 0.5, ((0, 64),)),
        "down_blocks": noise(keys[4], (NB, BLK, BLK), BLK ** -0.5, 0.5, ((0, 64),)),
        "col_block": draw_col_block(jax.random.fold_in(keys[8], 71), 0),
        "in_row": draw_in_row(jax.random.fold_in(keys[8], 71), 0),
        "out_row": draw_out_row(jax.random.fold_in(keys[8], 71), 0),
    }


def reference(tokens, cotangent, gate_blocks, up_blocks, down_blocks, col_block, in_row, out_row):
    highest = lax.Precision.HIGHEST
    row_blocks = D // BLK
    owned_cols = FF // (BLK * N_MP)
    owner_of = col_block // owned_cols
    same_column = (col_block[:, None] == col_block[None, :]).astype(jnp.float32)
    owner_onehot = (owner_of[None, :] == jnp.arange(N_MP, dtype=jnp.int32)[:, None]).astype(jnp.float32)
    row_onehot = (in_row[:, None] == jnp.arange(row_blocks, dtype=jnp.int32)[None, :]).astype(jnp.float32)
    gate_full = gate_blocks.astype(jnp.float32)
    up_full = up_blocks.astype(jnp.float32)
    down_full = down_blocks.astype(jnp.float32)
    groups = TOKENS // TOK_DEV
    token_groups = tokens.reshape(groups, TOK_DEV, row_blocks, BLK)
    cot_groups = cotangent.reshape(groups, TOK_DEV, row_blocks, BLK)

    def one_group(totals, tiles):
        token_tile, cot_tile = tiles
        token_in = jnp.take(token_tile, in_row, axis=1).astype(jnp.float32)
        cot_in = jnp.take(cot_tile, out_row, axis=1).astype(jnp.float32)
        gate_part = jnp.einsum('tkb,kbc->ktc', token_in, gate_full, precision=highest)
        up_part = jnp.einsum('tkb,kbc->ktc', token_in, up_full, precision=highest)
        gate_total = jnp.einsum('jk,ktc->jtc', same_column, gate_part, precision=highest)
        up_total = jnp.einsum('jk,ktc->jtc', same_column, up_part, precision=highest)
        gate_sigmoid = jax.nn.sigmoid(gate_total)
        gate_act = gate_total * gate_sigmoid
        hidden = (gate_act * up_total).astype(jnp.bfloat16)
        down_part = jnp.einsum('tkb,kcb->ktc', cot_in, down_full, precision=highest)
        hidden_grad = jnp.einsum('jk,ktc->jtc', same_column, down_part, precision=highest)
        gate_grad = (hidden_grad * up_total * gate_sigmoid * (1.0 + gate_total * (1.0 - gate_sigmoid))).astype(jnp.bfloat16)
        up_grad = (hidden_grad * gate_act).astype(jnp.bfloat16)
        down_term = jnp.einsum('ktc,tkb->kcb', hidden.astype(jnp.float32), cot_in, precision=highest)
        gate_term = jnp.einsum('tkb,ktc->kbc', token_in, gate_grad.astype(jnp.float32), precision=highest)
        up_term = jnp.einsum('tkb,ktc->kbc', token_in, up_grad.astype(jnp.float32), precision=highest)
        spread = jnp.einsum('ktc,kbc->ktb', gate_grad.astype(jnp.float32), gate_full, precision=highest)
        spread = spread + jnp.einsum('ktc,kbc->ktb', up_grad.astype(jnp.float32), up_full, precision=highest)
        owner_parts = jnp.einsum('mk,kr,ktb->mtrb', owner_onehot, row_onehot, spread, precision=highest)
        rounded = lax.optimization_barrier(owner_parts.astype(jnp.bfloat16)).astype(jnp.float32)
        input_tile = jnp.sum(rounded, axis=0).astype(jnp.bfloat16).reshape(TOK_DEV, D)
        return (totals[0] + gate_term, totals[1] + up_term, totals[2] + down_term), input_tile

    zeros_grad = jnp.zeros((NB, BLK, BLK), jnp.float32)
    totals, input_tiles = lax.scan(one_group, (zeros_grad, zeros_grad, zeros_grad), (token_groups, cot_groups))
    grad_scale = TOKENS ** -0.5
    return (input_tiles.reshape(TOKENS, D), totals[0] * grad_scale, totals[1] * grad_scale, totals[2] * grad_scale)
```

```python
import jax
import jax.numpy as jnp
from jax import lax
from jax.experimental import pallas as pl
from jax.experimental.pallas import tpu as pltpu
from jax.sharding import Mesh
from jax.sharding import PartitionSpec as P

AXES = ("zh", "y", "c", "x", "zl")
SIZE = {"zh": 4, "y": 8, "c": 2, "x": 4, "zl": 2}
BLK = 128
TOK = 144
D = 4096
NB = 64
SUB = 16
MESH_ID = pl.DeviceIdType.MESH
F32, BF16 = jnp.float32, jnp.bfloat16
Y_OFF = (4, 3, 5, 2, 6, 1, 7)
Z_OFF = (2, 1, 3)
MP_OFF = ((2, 0), (2, 1), (1, 0), (3, 0), (1, 1), (3, 1), (0, 1))


def at(axis, offset):
    return lax.rem(lax.axis_index(axis) + (SIZE[axis] + offset), SIZE[axis])


def sibling():
    return {"c": 1 - lax.axis_index("c")}


def mp_peer(off):
    return {"x": at("x", off[0]), "zl": at("zl", off[1])}


def enter(devices):
    barrier = pltpu.get_barrier_semaphore()
    for d in devices:
        pl.semaphore_signal(barrier, inc=1, device_id=d, device_id_type=MESH_ID)
    pl.semaphore_wait(barrier, len(devices))


def send(src, dst, s, r, device):
    copy = pltpu.make_async_remote_copy(
        src_ref=src, dst_ref=dst, send_sem=s, recv_sem=r, device_id=device, device_id_type=MESH_ID
    )
    copy.start()
    return copy


def gather_kernel(gate, up, down, a_out, b_out, own_a, own_b, tg, tu, s_sem, r_sem, s_sib, r_sib):
    c, z, y = lax.axis_index("c"), lax.axis_index("zh"), lax.axis_index("y")
    rows = pl.ds((lax.axis_index("x") * 2 + lax.axis_index("zl")) * SUB, SUB)
    tg[...] = gate[0].astype(F32).T
    tu[...] = up[0].astype(F32).T
    own_a[0:SUB] = tg[rows].astype(BF16)
    own_a[SUB:] = tu[rows].astype(BF16)
    own_b[...] = down[0, rows]
    a_out[c, y, z] = own_a[...]
    b_out[c, z, y] = own_b[...]
    enter([{"zh": at("zh", o)} for o in Z_OFF] + [{"y": at("y", o)} for o in Y_OFF] + [sibling()])
    a1 = [
        send(own_a, a_out.at[c, y, z], s_sem.at[o], r_sem.at[o], {"zh": at("zh", o)})
        for o in Z_OFF
    ]
    b1 = [
        send(own_b, b_out.at[c, z, y], s_sem.at[8 + o], r_sem.at[8 + o], {"y": at("y", o)})
        for o in Y_OFF
    ]
    for copy in a1:
        copy.wait_recv()
    a2 = [
        send(a_out.at[c, y], a_out.at[c, y], s_sem.at[16 + o], r_sem.at[16 + o], {"y": at("y", o)})
        for o in Y_OFF
    ]
    for copy in b1:
        copy.wait_recv()
    b2 = [
        send(b_out.at[c, z], b_out.at[c, z], s_sem.at[4 + o], r_sem.at[4 + o], {"zh": at("zh", o)})
        for o in Z_OFF
    ]
    shared = []

    def share(ref, index, slot):
        part = ref.at[c, index]
        shared.append(send(part, part, s_sib.at[slot], r_sib.at[slot], sibling()))

    share(a_out, y, 0)
    share(b_out, z, 8)
    for o, copy in list(zip(Y_OFF, a2))[::-1][:4]:
        copy.wait_recv()
        share(a_out, at("y", -o), o)
    for o, copy in list(zip(Z_OFF, b2))[::-1]:
        copy.wait_recv()
        share(b_out, at("zh", -o), 8 + o)
    for o, copy in list(zip(Y_OFF, a2))[:3][::-1]:
        copy.wait_recv()
        share(a_out, at("y", -o), o)
    for copy in shared:
        copy.wait()
    for copy in a1 + b1 + a2 + b2:
        copy.wait_send()


def gathered(gate, up, down):
    vmem = pl.BlockSpec(memory_space=pltpu.VMEM)
    return pl.pallas_call(
        gather_kernel,
        name="gather_blocks",
        out_shape=(
            jax.ShapeDtypeStruct((2, 8, 4, 2 * SUB, BLK), BF16),
            jax.ShapeDtypeStruct((2, 4, 8, SUB, BLK), BF16),
        ),
        in_specs=[vmem] * 3,
        out_specs=(vmem, vmem),
        scratch_shapes=[
            pltpu.VMEM((2 * SUB, BLK), BF16),
            pltpu.VMEM((SUB, BLK), BF16),
            pltpu.VMEM((BLK, BLK), F32),
            pltpu.VMEM((BLK, BLK), F32),
            pltpu.SemaphoreType.DMA((24,)),
            pltpu.SemaphoreType.DMA((24,)),
            pltpu.SemaphoreType.DMA((12,)),
            pltpu.SemaphoreType.DMA((12,)),
        ],
        compiler_params=pltpu.CompilerParams(
            collective_id=0, has_side_effects=True, vmem_limit_bytes=32 << 20
        ),
    )(gate, up, down)


def flat_of(p):
    return (p % 4) * 16 + ((p // 4) % 8) * 2 + p // 32


def place_of(k):
    return (k % 2) * 32 + ((k // 2) % 8) * 4 + k // 16


def dot_nt(a, b):
    return lax.dot_general(a, b, (((1,), (1,)), ((), ())), preferred_element_type=F32)


def dot(a, b):
    return jnp.dot(a, b, preferred_element_type=F32)


def compute_kernel(slot, in_row, out_row, tok, cot, a, b, part, wa, wb, w, dn, g_s, u_s, h_s, acc):
    def columns(ref, row):
        return ref[:, pl.ds(pl.multiple_of(row * BLK, BLK), BLK)]

    w[...] = jnp.zeros_like(w)
    dn[...] = jnp.zeros_like(dn)
    acc[...] = jnp.zeros_like(acc)

    @pl.loop(0, 8)
    def _(t):
        xs, ys = [], []
        for i in range(8):
            core, yy, zz = t // 4, (t % 4) * 2 + i // 4, i % 4
            k = zz * 16 + yy * 2 + core
            lanes = slice(i * BLK, (i + 1) * BLK)
            w[t, i * SUB : (i + 1) * SUB, lanes] = a[core, yy, zz, 0:SUB]
            w[t, BLK + i * SUB : BLK + (i + 1) * SUB, lanes] = a[core, yy, zz, SUB:]
            dn[t, i * SUB : (i + 1) * SUB, lanes] = b[core, zz, yy]
            xs.append(columns(tok, in_row[k]))
            ys.append(columns(cot, out_row[k]))
        gu = dot_nt(jnp.concatenate(xs, axis=1), w[t])
        g_s[t] = gu[:, :BLK]
        u_s[t] = gu[:, BLK:]
        h_s[t] = dot_nt(jnp.concatenate(ys, axis=1), dn[t])

    group = lax.broadcasted_iota(jnp.int32, (TOK, BLK), 1) // SUB

    @pl.loop(0, NB)
    def _(p):
        k = flat_of(p)

        @pl.when(slot[k] != k)
        def _():
            q = place_of(slot[k])
            shift = lax.rem((q - p) * SUB + 16 * BLK, BLK)
            for s in (g_s, u_s, h_s):
                moved = pltpu.roll(s[p // 8], shift, axis=1)
                s[q // 8] += jnp.where(group == q % 8, moved, 0.0)

    @pl.loop(0, NB)
    def _(p):
        k = flat_of(p)

        @pl.when(slot[k] != k)
        def _():
            q = place_of(slot[k])
            shift = lax.rem((p - q) * SUB + 16 * BLK, BLK)
            for s in (g_s, u_s, h_s):
                moved = pltpu.roll(s[q // 8], shift, axis=1)
                s[p // 8] = jnp.where(group == p % 8, moved, s[p // 8])

    @pl.loop(0, 8)
    def _(t):
        gate, up, hg = g_s[t], u_s[t], h_s[t]
        sig = jax.nn.sigmoid(gate)
        act = gate * sig
        hid = (act * up).T.astype(BF16)
        gg = hg * up * sig * (1.0 + gate * (1.0 - sig))
        ug = hg * act
        ggt, ugt = gg.T.astype(BF16), ug.T.astype(BF16)
        spread = dot(jnp.concatenate([gg.astype(BF16), ug.astype(BF16)], axis=1), w[t])
        for i in range(8):
            core, yy, zz = t // 4, (t % 4) * 2 + i // 4, i % 4
            k = zz * 16 + yy * 2 + core
            acc[in_row[k]] += spread[:, i * BLK : (i + 1) * BLK]
        for j in range(4):
            rows = slice(32 * j, 32 * j + 32)
            idx = []
            for i in (2 * j, 2 * j + 1):
                idx.append((t // 4, (t % 4) * 2 + i // 4, i % 4))
            ks = [zz * 16 + yy * 2 + core for core, yy, zz in idx]
            left = jnp.concatenate([ggt[rows], ugt[rows]], axis=0)
            r = dot(left, jnp.concatenate([columns(tok, in_row[k]) for k in ks], axis=1))
            d = dot(hid[rows], jnp.concatenate([columns(cot, out_row[k]) for k in ks], axis=1))
            for n, (core, yy, zz) in enumerate(idx):
                lanes = slice(n * BLK, (n + 1) * BLK)
                wa[core, yy, zz, 0:SUB] = r[n * SUB : (n + 1) * SUB, lanes]
                wa[core, yy, zz, SUB:] = r[32 + n * SUB : 32 + (n + 1) * SUB, lanes]
                wb[core, zz, yy] = d[n * SUB : (n + 1) * SUB, lanes]

    for m in range(8):
        for j in range(4):
            part[m, :, j * BLK : (j + 1) * BLK] = acc[4 * m + j].astype(BF16)


def computed(slot, in_row, out_row, tok, cot, a, b):
    vmem = pl.BlockSpec(memory_space=pltpu.VMEM)
    smem = pl.BlockSpec(memory_space=pltpu.SMEM)
    return pl.pallas_call(
        compute_kernel,
        name="block_grads",
        out_shape=(
            jax.ShapeDtypeStruct((8, TOK, 512), BF16),
            jax.ShapeDtypeStruct((2, 8, 4, 2 * SUB, BLK), F32),
            jax.ShapeDtypeStruct((2, 4, 8, SUB, BLK), F32),
        ),
        in_specs=[smem] * 3 + [vmem] * 4,
        out_specs=(vmem,) * 3,
        scratch_shapes=[
            pltpu.VMEM((8, 256, 1024), BF16),
            pltpu.VMEM((8, 128, 1024), BF16),
            pltpu.VMEM((8, TOK, BLK), F32),
            pltpu.VMEM((8, TOK, BLK), F32),
            pltpu.VMEM((8, TOK, BLK), F32),
            pltpu.VMEM((32, TOK, BLK), F32),
        ],
        compiler_params=pltpu.CompilerParams(vmem_limit_bytes=48 << 20),
    )(slot, in_row, out_row, tok, cot, a, b)


def reduce_kernel(
    part, wa, wb, ig_out, g_out, u_out, d_out,
    ig_in, sib_a, sib_b, sum_a, sum_b, in_a1, in_b1, sum_a2, sum_b2, in_a2, in_b2, fin,
    s_sem, r_sem, s_mp, r_mp, s_fin, r_fin,
):
    c, z, y = lax.axis_index("c"), lax.axis_index("zh"), lax.axis_index("y")
    x, zl = lax.axis_index("x"), lax.axis_index("zl")
    m = x * 2 + zl
    enter(
        [{"zh": at("zh", o)} for o in Z_OFF]
        + [{"y": at("y", o)} for o in Y_OFF]
        + [sibling()]
        + [mp_peer(o) for o in MP_OFF]
    )
    o = 1 - c
    sib = [
        send(wa.at[o], sib_a, s_sem.at[0], r_sem.at[0], sibling()),
        send(wb.at[o], sib_b, s_sem.at[8], r_sem.at[8], sibling()),
    ]
    exch = []
    for i, off in enumerate(MP_OFF):
        peer = mp_peer(off)
        exch.append(
            send(part.at[peer["x"] * 2 + peer["zl"]], ig_in.at[i], s_mp.at[i], r_mp.at[i], peer)
        )
    sib[0].wait_recv()
    sum_a[...] = (wa[c] + sib_a[...]).astype(BF16)
    a1 = []
    for off in Y_OFF:
        q = at("y", off)
        a1.append(
            send(sum_a.at[q], in_a1.at[off], s_sem.at[16 + off], r_sem.at[16 + off], {"y": q})
        )
    sib[1].wait_recv()
    sum_b[...] = (wb[c] + sib_b[...]).astype(BF16)
    b1 = []
    for off in Z_OFF:
        q = at("zh", off)
        b1.append(
            send(sum_b.at[q], in_b1.at[off], s_sem.at[4 + off], r_sem.at[4 + off], {"zh": q})
        )
    total = sum_b[z].astype(F32)
    for off, copy in zip(Z_OFF, b1):
        copy.wait_recv()
        total += in_b1[off].astype(F32)
    sum_b2[...] = total.astype(BF16)
    b2 = []
    for off in Y_OFF:
        q = at("y", off)
        b2.append(
            send(sum_b2.at[q], in_b2.at[off], s_sem.at[8 + off], r_sem.at[8 + off], {"y": q})
        )
    total = sum_a[y].astype(F32)
    for off, copy in zip(Y_OFF, a1):
        copy.wait_recv()
        total += in_a1[off].astype(F32)
    sum_a2[...] = total.astype(BF16)
    a2 = []
    for off in Z_OFF:
        q = at("zh", off)
        a2.append(send(sum_a2.at[q], in_a2.at[off], s_sem.at[off], r_sem.at[off], {"zh": q}))
    total = sum_b2[y].astype(F32)
    for off, copy in zip(Y_OFF, b2):
        copy.wait_recv()
        total += in_b2[off].astype(F32)
    fin[m, 2 * SUB :] = total
    total = sum_a2[z].astype(F32)
    for off, copy in zip(Z_OFF, a2):
        copy.wait_recv()
        total += in_a2[off].astype(F32)
    fin[m, 0 : 2 * SUB] = total
    last = [
        send(fin.at[m], fin.at[m], s_fin.at[i], r_fin.at[i], mp_peer(off))
        for i, off in enumerate(MP_OFF)
    ]
    total = part[m].astype(F32)
    for i, copy in enumerate(exch):
        copy.wait_recv()
        total += ig_in[i].astype(F32)
    ig_out[...] = total.astype(BF16)
    for copy in last:
        copy.wait_recv()
    scale = 9216**-0.5
    g_out[0] = fin[:, 0:SUB].reshape(BLK, BLK).T * scale
    u_out[0] = fin[:, SUB : 2 * SUB].reshape(BLK, BLK).T * scale
    d_out[0] = fin[:, 2 * SUB :].reshape(BLK, BLK) * scale
    for copy in sib + exch + a1 + b1 + a2 + b2 + last:
        copy.wait_send()


def reduced(part, wa, wb):
    vmem = pl.BlockSpec(memory_space=pltpu.VMEM)
    grad = jax.ShapeDtypeStruct((1, BLK, BLK), F32)
    return pl.pallas_call(
        reduce_kernel,
        name="sum_grads",
        out_shape=(jax.ShapeDtypeStruct((TOK, 512), BF16), grad, grad, grad),
        in_specs=[vmem] * 3,
        out_specs=(vmem,) * 4,
        scratch_shapes=[
            pltpu.VMEM((7, TOK, 512), BF16),
            pltpu.VMEM((8, 4, 2 * SUB, BLK), F32),
            pltpu.VMEM((4, 8, SUB, BLK), F32),
            pltpu.VMEM((8, 4, 2 * SUB, BLK), BF16),
            pltpu.VMEM((4, 8, SUB, BLK), BF16),
            pltpu.VMEM((8, 4, 2 * SUB, BLK), BF16),
            pltpu.VMEM((4, 8, SUB, BLK), BF16),
            pltpu.VMEM((4, 2 * SUB, BLK), BF16),
            pltpu.VMEM((8, SUB, BLK), BF16),
            pltpu.VMEM((4, 2 * SUB, BLK), BF16),
            pltpu.VMEM((8, SUB, BLK), BF16),
            pltpu.VMEM((8, 3 * SUB, BLK), F32),
            pltpu.SemaphoreType.DMA((24,)),
            pltpu.SemaphoreType.DMA((24,)),
            pltpu.SemaphoreType.DMA((7,)),
            pltpu.SemaphoreType.DMA((7,)),
            pltpu.SemaphoreType.DMA((7,)),
            pltpu.SemaphoreType.DMA((7,)),
        ],
        compiler_params=pltpu.CompilerParams(
            collective_id=1, has_side_effects=True, vmem_limit_bytes=32 << 20
        ),
    )(part, wa, wb)


def on_device(tokens, cotangent, gate, up, down, col_block, in_row, out_row):
    slot = jnp.argmax(col_block[:, None] == col_block[None, :], axis=1).astype(jnp.int32)
    a, b = gathered(gate, up, down)
    part, wa, wb = computed(slot, in_row, out_row, tokens, cotangent, a, b)
    return reduced(part, wa, wb)


def solution(mesh):
    fine = Mesh(mesh.devices.reshape(4, 8, 2, 4, 2), AXES)
    dp, mp = ("zh", "y", "c"), ("x", "zl")
    return jax.shard_map(
        on_device,
        mesh=fine,
        in_specs=(P(dp, None), P(dp, None), P(dp), P(dp), P(dp), P(), P(), P()),
        out_specs=(P(dp, mp), P(dp), P(dp), P(dp)),
        check_vma=False,
    )
```

```python
import jax
import jax.numpy as jnp
from jax import lax
from jax.experimental import pallas as pl
from jax.experimental.pallas import tpu as pltpu
from jax.sharding import Mesh
from jax.sharding import PartitionSpec as P

AXES = ("zh", "y", "c", "x", "zl")
SIZE = {"zh": 4, "y": 8, "c": 2, "x": 4, "zl": 2}
BLK = 128
TOK = 144
D = 4096
NB = 64
SUB = 16
MESH_ID = pl.DeviceIdType.MESH
F32, BF16 = jnp.float32, jnp.bfloat16
Y_OFF = (4, 3, 5, 2, 6, 1, 7)
Z_OFF = (2, 1, 3)
X_OFF = (2, 1, 3)
MP_OFF = ((2, 0), (2, 1), (1, 0), (3, 0), (1, 1), (3, 1), (0, 1))


def at(axis, offset):
    return lax.rem(lax.axis_index(axis) + (SIZE[axis] + offset), SIZE[axis])


def sibling():
    return {"c": 1 - lax.axis_index("c")}


def mp_peer(off):
    return {"x": at("x", off[0]), "zl": at("zl", off[1])}


def enter(devices):
    barrier = pltpu.get_barrier_semaphore()
    for d in devices:
        pl.semaphore_signal(barrier, inc=1, device_id=d, device_id_type=MESH_ID)
    pl.semaphore_wait(barrier, len(devices))


def send(src, dst, s, r, device):
    copy = pltpu.make_async_remote_copy(
        src_ref=src, dst_ref=dst, send_sem=s, recv_sem=r, device_id=device, device_id_type=MESH_ID
    )
    copy.start()
    return copy


def gather_kernel(
    gate, up, down, tok, cot, col, in_row, out_row,
    w, dn, tok_v, cot_v, meta,
    a_in, b_in, own_a, own_b, raw, lists, s_sem, r_sem, s_sib, r_sib, local,
):
    c, z, y = lax.axis_index("c"), lax.axis_index("zh"), lax.axis_index("y")
    rows = pl.ds((lax.axis_index("x") * 2 + lax.axis_index("zl")) * SUB, SUB)
    partners = (
        [{"zh": at("zh", o)} for o in Z_OFF] + [{"y": at("y", o)} for o in Y_OFF] + [sibling()]
    )
    barrier = pltpu.get_barrier_semaphore()
    for d in partners:
        pl.semaphore_signal(barrier, inc=1, device_id=d, device_id_type=MESH_ID)
    meta[...] = jnp.zeros_like(meta)
    loads = [
        pltpu.make_async_copy(src, dst, local.at[i])
        for i, (src, dst) in enumerate(
            (
                (gate.at[0], raw.at[0]),
                (up.at[0], raw.at[1]),
                (down.at[0, rows], own_b),
                (col, lists.at[0]),
                (in_row, lists.at[1]),
                (out_row, lists.at[2]),
                (tok, tok_v),
                (cot, cot_v),
            )
        )
    ]
    for copy in loads:
        copy.start()
    for i in range(2):
        loads[i].wait()
    turned = [raw[i].astype(F32).T.astype(BF16) for i in range(2)]
    for i in range(2):
        raw[i] = turned[i]
    for i in range(2):
        own_a[i * SUB : (i + 1) * SUB] = raw[i, rows]
    loads[2].wait()
    a_in[c, y, z] = own_a[...]
    b_in[c, z, y] = own_b[...]
    pl.semaphore_wait(barrier, len(partners))
    a1 = [
        send(own_a, a_in.at[c, y, z], s_sem.at[o], r_sem.at[o], {"zh": at("zh", o)})
        for o in Z_OFF
    ]
    b1 = [
        send(own_b, b_in.at[c, z, y], s_sem.at[8 + o], r_sem.at[8 + o], {"y": at("y", o)})
        for o in Y_OFF
    ]
    for copy in a1:
        copy.wait_recv()
    a2 = [
        send(a_in.at[c, y], a_in.at[c, y], s_sem.at[16 + o], r_sem.at[16 + o], {"y": at("y", o)})
        for o in Y_OFF
    ]
    for copy in b1:
        copy.wait_recv()
    b2 = [
        send(b_in.at[c, z], b_in.at[c, z], s_sem.at[4 + o], r_sem.at[4 + o], {"zh": at("zh", o)})
        for o in Z_OFF
    ]
    shared = []

    def share(ref, index, slot):
        part = ref.at[c, index]
        shared.append(send(part, part, s_sib.at[slot], r_sib.at[slot], sibling()))

    share(a_in, y, 0)
    share(b_in, z, 8)

    @pl.loop(0, 8)
    def _(t):
        w[t] = jnp.zeros_like(w[t])
        dn[t] = jnp.zeros_like(dn[t])

    for copy in loads[3:]:
        copy.wait()
    meta[0:3, 0:NB] = lists[...]
    across = jnp.broadcast_to(meta[0:1].astype(F32), (BLK, BLK))
    order = lax.broadcasted_iota(jnp.int32, (BLK, BLK), 0)
    meta[3:4] = jnp.min(jnp.where(across == across.T, order, NB), axis=0, keepdims=True)

    for o, copy in list(zip(Y_OFF, a2))[::-1][:4]:
        copy.wait_recv()
        share(a_in, at("y", -o), o)
    for o, copy in list(zip(Z_OFF, b2))[::-1]:
        copy.wait_recv()
        share(b_in, at("zh", -o), 8 + o)
    for o, copy in list(zip(Y_OFF, a2))[:3][::-1]:
        copy.wait_recv()
        share(a_in, at("y", -o), o)
    for copy in shared:
        copy.wait()

    @pl.loop(0, 8)
    def _(t):
        for i in range(8):
            core, yy, zz = t // 4, (t % 4) * 2 + i // 4, i % 4
            lanes = slice(i * BLK, (i + 1) * BLK)
            w[t, i * SUB : (i + 1) * SUB, lanes] = a_in[core, yy, zz, 0:SUB]
            w[t, BLK + i * SUB : BLK + (i + 1) * SUB, lanes] = a_in[core, yy, zz, SUB:]
            dn[t, i * SUB : (i + 1) * SUB, lanes] = b_in[core, zz, yy]

    for copy in a1 + b1 + a2 + b2:
        copy.wait_send()


def gathered(*args):
    hbm = pl.BlockSpec(memory_space=pltpu.HBM)
    vmem = pl.BlockSpec(memory_space=pltpu.VMEM)
    return pl.pallas_call(
        gather_kernel,
        name="gather_blocks",
        out_shape=(
            jax.ShapeDtypeStruct((8, 256, 1024), BF16),
            jax.ShapeDtypeStruct((8, 128, 1024), BF16),
            jax.ShapeDtypeStruct((TOK, D), BF16),
            jax.ShapeDtypeStruct((TOK, D), BF16),
            jax.ShapeDtypeStruct((8, BLK), jnp.int32),
        ),
        in_specs=[hbm] * 8,
        out_specs=(vmem,) * 5,
        scratch_shapes=[
            pltpu.VMEM((2, 8, 4, 2 * SUB, BLK), BF16),
            pltpu.VMEM((2, 4, 8, SUB, BLK), BF16),
            pltpu.VMEM((2 * SUB, BLK), BF16),
            pltpu.VMEM((SUB, BLK), BF16),
            pltpu.VMEM((2, BLK, BLK), BF16),
            pltpu.VMEM((3, NB), jnp.int32),
            pltpu.SemaphoreType.DMA((24,)),
            pltpu.SemaphoreType.DMA((24,)),
            pltpu.SemaphoreType.DMA((12,)),
            pltpu.SemaphoreType.DMA((12,)),
            pltpu.SemaphoreType.DMA((8,)),
        ],
        compiler_params=pltpu.CompilerParams(
            collective_id=0, has_side_effects=True, vmem_limit_bytes=32 << 20
        ),
    )(*args)


def place_of(k):
    return ((k & 1) << 5) | (((k >> 1) & 7) << 2) | (k >> 4)


def dot_nt(a, b):
    return lax.dot_general(a, b, (((1,), (1,)), ((), ())), preferred_element_type=F32)


def dot(a, b):
    return jnp.dot(a, b, preferred_element_type=F32)


def compute_kernel(
    w, dn, tok, cot, meta, part, wa, wb, acc, g_s, u_s, h_s, table, pairs, sem
):
    load = pltpu.make_async_copy(meta, table, sem)
    load.start()
    load.wait()

    def columns(ref, row):
        return ref[:, pl.ds(pl.multiple_of(row * BLK, BLK), BLK)]

    def flat(t, i):
        return (i % 4) * 16 + (((t & 3) * 2 + i // 4) * 2) + (t >> 2)

    @pl.loop(0, 8)
    def _(t):
        acc[pl.ds(t * 4, 4)] = jnp.zeros((4, TOK, BLK), F32)
        ks = [flat(t, i) for i in range(8)]
        gu = dot_nt(jnp.concatenate([columns(tok, table[1, k]) for k in ks], axis=1), w[t])
        g_s[t] = gu[:, :BLK]
        u_s[t] = gu[:, BLK:]
        h_s[t] = dot_nt(jnp.concatenate([columns(cot, table[2, k]) for k in ks], axis=1), dn[t])

    count = jnp.int32(0)
    for k in range(NB):
        first = table[3, k]
        pairs[count] = place_of(k) | (place_of(first) << 8)
        count = count + (first != k).astype(jnp.int32)
    group = lax.broadcasted_iota(jnp.int32, (TOK, BLK), 1) // SUB

    @pl.loop(0, count)
    def _(n):
        p, q = pairs[n] & 255, pairs[n] >> 8
        shift = ((q - p) * SUB) & (BLK - 1)
        for s in (g_s, u_s, h_s):
            moved = pltpu.roll(s[p >> 3], shift, axis=1)
            s[q >> 3] += jnp.where(group == (q & 7), moved, 0.0)

    @pl.loop(0, count)
    def _(n):
        p, q = pairs[n] & 255, pairs[n] >> 8
        shift = ((p - q) * SUB) & (BLK - 1)
        for s in (g_s, u_s, h_s):
            moved = pltpu.roll(s[q >> 3], shift, axis=1)
            s[p >> 3] = jnp.where(group == (p & 7), moved, s[p >> 3])

    @pl.loop(0, 8)
    def _(t):
        gate, up, hg = g_s[t], u_s[t], h_s[t]
        sig = jax.nn.sigmoid(gate)
        act = gate * sig
        hid = (act * up).T.astype(BF16)
        gg = hg * up * sig * (1.0 + gate * (1.0 - sig))
        ug = hg * act
        ggt, ugt = gg.T.astype(BF16), ug.T.astype(BF16)
        spread = dot(jnp.concatenate([gg.astype(BF16), ug.astype(BF16)], axis=1), w[t])
        for i in range(8):
            acc[table[1, flat(t, i)]] += spread[:, i * BLK : (i + 1) * BLK]
        core = t >> 2
        for j in range(4):
            rows = slice(32 * j, 32 * j + 32)
            ks = [flat(t, 2 * j), flat(t, 2 * j + 1)]
            left = jnp.concatenate([ggt[rows], ugt[rows]], axis=0)
            r = dot(left, jnp.concatenate([columns(tok, table[1, k]) for k in ks], axis=1))
            d = dot(hid[rows], jnp.concatenate([columns(cot, table[2, k]) for k in ks], axis=1))
            for n in range(2):
                i = 2 * j + n
                yy, zz = (t & 3) * 2 + i // 4, i % 4
                lanes = slice(n * BLK, (n + 1) * BLK)
                wa[core, yy, zz, 0:SUB] = r[n * SUB : (n + 1) * SUB, lanes]
                wa[core, yy, zz, SUB:] = r[32 + n * SUB : 32 + (n + 1) * SUB, lanes]
                wb[core, zz, yy] = d[n * SUB : (n + 1) * SUB, lanes]

    for m in range(8):
        for j in range(4):
            part[m, :, j * BLK : (j + 1) * BLK] = acc[4 * m + j].astype(BF16)


def computed(*args):
    vmem = pl.BlockSpec(memory_space=pltpu.VMEM)
    return pl.pallas_call(
        compute_kernel,
        name="block_grads",
        out_shape=(
            jax.ShapeDtypeStruct((8, TOK, 512), BF16),
            jax.ShapeDtypeStruct((2, 8, 4, 2 * SUB, BLK), F32),
            jax.ShapeDtypeStruct((2, 4, 8, SUB, BLK), F32),
        ),
        in_specs=[vmem] * 5,
        out_specs=(vmem,) * 3,
        scratch_shapes=[
            pltpu.VMEM((32, TOK, BLK), F32),
            pltpu.VMEM((8, TOK, BLK), F32),
            pltpu.VMEM((8, TOK, BLK), F32),
            pltpu.VMEM((8, TOK, BLK), F32),
            pltpu.SMEM((8, BLK), jnp.int32),
            pltpu.SMEM((BLK,), jnp.int32),
            pltpu.SemaphoreType.DMA,
        ],
        compiler_params=pltpu.CompilerParams(vmem_limit_bytes=24 << 20),
    )(*args)


def reduce_kernel(
    part, wa, wb, ig_in, fin,
    mid, sib_a, sib_b, sum_a, sum_b, in_a1, in_b1, sum_a2, sum_b2, in_a2, in_b2,
    s_sem, r_sem, s_mp, r_mp, s_fin, r_fin,
):
    c, z, y = lax.axis_index("c"), lax.axis_index("zh"), lax.axis_index("y")
    x, zl = lax.axis_index("x"), lax.axis_index("zl")
    m = x * 2 + zl
    enter(
        [{"zh": at("zh", o)} for o in Z_OFF]
        + [{"y": at("y", o)} for o in Y_OFF]
        + [sibling()]
        + [mp_peer(o) for o in MP_OFF]
    )
    o = 1 - c
    sib = [
        send(wa.at[o], sib_a, s_sem.at[0], r_sem.at[0], sibling()),
        send(wb.at[o], sib_b, s_sem.at[8], r_sem.at[8], sibling()),
    ]
    exch = []
    for h in range(2):
        for i, off in enumerate(X_OFF):
            q = at("x", off)
            n = h * 3 + i
            chunk = q * 2 + (1 - zl if h == 0 else zl)
            exch.append(send(part.at[chunk], ig_in.at[n], s_mp.at[n], r_mp.at[n], {"x": q}))
    sib[0].wait_recv()
    sum_a[...] = (wa[c] + sib_a[...]).astype(BF16)
    a1 = []
    for off in Y_OFF:
        q = at("y", off)
        a1.append(
            send(sum_a.at[q], in_a1.at[off], s_sem.at[16 + off], r_sem.at[16 + off], {"y": q})
        )
    sib[1].wait_recv()
    sum_b[...] = (wb[c] + sib_b[...]).astype(BF16)
    b1 = []
    for off in Z_OFF:
        q = at("zh", off)
        b1.append(
            send(sum_b.at[q], in_b1.at[off], s_sem.at[4 + off], r_sem.at[4 + off], {"zh": q})
        )
    total = sum_b[z].astype(F32)
    for off, copy in zip(Z_OFF, b1):
        copy.wait_recv()
        total += in_b1[off].astype(F32)
    sum_b2[...] = total.astype(BF16)
    b2 = []
    for off in Y_OFF:
        q = at("y", off)
        b2.append(
            send(sum_b2.at[q], in_b2.at[off], s_sem.at[8 + off], r_sem.at[8 + off], {"y": q})
        )
    total = sum_a[y].astype(F32)
    for off, copy in zip(Y_OFF, a1):
        copy.wait_recv()
        total += in_a1[off].astype(F32)
    sum_a2[...] = total.astype(BF16)
    a2 = []
    for off in Z_OFF:
        q = at("zh", off)
        a2.append(send(sum_a2.at[q], in_a2.at[off], s_sem.at[off], r_sem.at[off], {"zh": q}))
    total = part[x * 2 + 1 - zl].astype(F32)
    for i in range(3):
        exch[i].wait_recv()
        total += ig_in[i].astype(F32)
    mid[...] = total.astype(BF16)
    exch.append(send(mid, ig_in.at[6], s_mp.at[6], r_mp.at[6], {"zl": 1 - zl}))
    total = sum_b2[y].astype(F32)
    for off, copy in zip(Y_OFF, b2):
        copy.wait_recv()
        total += in_b2[off].astype(F32)
    fin[m, 2 * SUB :] = total.astype(fin.dtype)
    total = sum_a2[z].astype(F32)
    for off, copy in zip(Z_OFF, a2):
        copy.wait_recv()
        total += in_a2[off].astype(F32)
    fin[m, 0 : 2 * SUB] = total.astype(fin.dtype)
    last = [
        send(fin.at[m], fin.at[m], s_fin.at[i], r_fin.at[i], mp_peer(off))
        for i, off in enumerate(MP_OFF)
    ]
    for copy in exch[3:] + last:
        copy.wait_recv()
    for copy in sib + exch + a1 + b1 + a2 + b2 + last:
        copy.wait_send()


def reduced(part, wa, wb):
    vmem = pl.BlockSpec(memory_space=pltpu.VMEM)
    return pl.pallas_call(
        reduce_kernel,
        name="sum_grads",
        out_shape=(
            jax.ShapeDtypeStruct((7, TOK, 512), BF16),
            jax.ShapeDtypeStruct((8, 3 * SUB, BLK), BF16),
        ),
        in_specs=[vmem] * 3,
        out_specs=(vmem,) * 2,
        scratch_shapes=[
            pltpu.VMEM((TOK, 512), BF16),
            pltpu.VMEM((8, 4, 2 * SUB, BLK), F32),
            pltpu.VMEM((4, 8, SUB, BLK), F32),
            pltpu.VMEM((8, 4, 2 * SUB, BLK), BF16),
            pltpu.VMEM((4, 8, SUB, BLK), BF16),
            pltpu.VMEM((8, 4, 2 * SUB, BLK), BF16),
            pltpu.VMEM((4, 8, SUB, BLK), BF16),
            pltpu.VMEM((4, 2 * SUB, BLK), BF16),
            pltpu.VMEM((8, SUB, BLK), BF16),
            pltpu.VMEM((4, 2 * SUB, BLK), BF16),
            pltpu.VMEM((8, SUB, BLK), BF16),
            pltpu.SemaphoreType.DMA((24,)),
            pltpu.SemaphoreType.DMA((24,)),
            pltpu.SemaphoreType.DMA((7,)),
            pltpu.SemaphoreType.DMA((7,)),
            pltpu.SemaphoreType.DMA((7,)),
            pltpu.SemaphoreType.DMA((7,)),
        ],
        compiler_params=pltpu.CompilerParams(
            collective_id=1, has_side_effects=True, vmem_limit_bytes=32 << 20
        ),
    )(part, wa, wb)


def finish_kernel(part, ig_in, fin, ig_out, g_out, u_out, d_out):
    total = part[lax.axis_index("x") * 2 + lax.axis_index("zl")].astype(F32)
    for i in range(3, 7):
        total += ig_in[i].astype(F32)
    ig_out[...] = total.astype(BF16)
    scale = 9216**-0.5
    g_out[0] = fin[:, 0:SUB].astype(F32).reshape(BLK, BLK).T * scale
    u_out[0] = fin[:, SUB : 2 * SUB].astype(F32).reshape(BLK, BLK).T * scale
    d_out[0] = fin[:, 2 * SUB :].astype(F32).reshape(BLK, BLK) * scale


def finished(part, ig_in, fin):
    vmem = pl.BlockSpec(memory_space=pltpu.VMEM)
    grad = jax.ShapeDtypeStruct((1, BLK, BLK), F32)
    return pl.pallas_call(
        finish_kernel,
        name="write_grads",
        out_shape=(jax.ShapeDtypeStruct((TOK, 512), BF16), grad, grad, grad),
        in_specs=[vmem] * 3,
        out_specs=(vmem,) * 4,
        compiler_params=pltpu.CompilerParams(vmem_limit_bytes=16 << 20),
    )(part, ig_in, fin)


def on_device(tokens, cotangent, gate, up, down, col_block, in_row, out_row):
    args = (gate, up, down, tokens, cotangent, col_block, in_row, out_row)
    tiles = gathered(*(pltpu.with_memory_space_constraint(a, pltpu.HBM) for a in args))
    part, wa, wb = computed(*tiles)
    return finished(part, *reduced(part, wa, wb))


def solution(mesh):
    fine = Mesh(mesh.devices.reshape(4, 8, 2, 4, 2), AXES)
    dp, mp = ("zh", "y", "c"), ("x", "zl")
    return jax.shard_map(
        on_device,
        mesh=fine,
        in_specs=(P(dp, None), P(dp, None), P(dp), P(dp), P(dp), P(), P(), P()),
        out_specs=(P(dp, mp), P(dp), P(dp), P(dp)),
        check_vma=False,
    )
```

```python
import jax
import jax.numpy as jnp
from jax import lax
from jax.experimental import pallas as pl
from jax.experimental.pallas import tpu as pltpu
from jax.sharding import Mesh
from jax.sharding import PartitionSpec as P

AXES = ("zh", "y", "c", "x", "zl")
SIZE = {"zh": 4, "y": 8, "c": 2, "x": 4, "zl": 2}
BLK = 128
TOK = 144
D = 4096
NB = 64
SUB = 16
MESH_ID = pl.DeviceIdType.MESH
F32, BF16 = jnp.float32, jnp.bfloat16
Y_OFF = (4, 3, 5, 2, 6, 1, 7)
Z_OFF = (2, 1, 3)
X_OFF = (2, 1, 3)
MP_OFF = ((2, 0), (2, 1), (1, 0), (3, 0), (1, 1), (3, 1), (0, 1))


def at(axis, offset):
    return lax.rem(lax.axis_index(axis) + (SIZE[axis] + offset), SIZE[axis])


def sibling():
    return {"c": 1 - lax.axis_index("c")}


def mp_peer(off):
    return {"x": at("x", off[0]), "zl": at("zl", off[1])}


def enter(devices):
    barrier = pltpu.get_barrier_semaphore()
    for d in devices:
        pl.semaphore_signal(barrier, inc=1, device_id=d, device_id_type=MESH_ID)
    pl.semaphore_wait(barrier, len(devices))


def send(src, dst, s, r, device):
    copy = pltpu.make_async_remote_copy(
        src_ref=src, dst_ref=dst, send_sem=s, recv_sem=r, device_id=device, device_id_type=MESH_ID
    )
    copy.start()
    return copy


OFF = {"y": Y_OFF, "zh": Z_OFF}
OTHER = {"y": "zh", "zh": "y"}
GATHER_FIRST = (("zh", "y"), ("y", "zh"))
REDUCE_FIRST = (("y", "zh"), ("zh", "y"))


def line(ref, axis, q):
    return ref.at[q] if axis == "y" else ref.at[pl.ds(0, SIZE["y"]), q]


def flat(t, i):
    return (i % 4) * 16 + (((t & 3) * 2 + i // 4) * 2) + (t >> 2)


def columns(ref, row):
    return ref[:, pl.ds(pl.multiple_of(row * BLK, BLK), BLK)]


def forward(t, tok, cot, in_row, out_row, w, dn):
    ks = [flat(t, i) for i in range(8)]
    gu = dot_nt(jnp.concatenate([columns(tok, in_row(k)) for k in ks], axis=1), w[t])
    hg = dot_nt(jnp.concatenate([columns(cot, out_row(k)) for k in ks], axis=1), dn[t])
    return gu[:, :BLK], gu[:, BLK:], hg


def gather_kernel(
    gate, up, down, tok, cot, col, in_row, out_row,
    w, dn, tok_v, cot_v, meta,
    a_in, b_in, own_a, own_b, raw, lists, s_sem, r_sem, s_sib, r_sib, local,
):
    c, z, y = lax.axis_index("c"), lax.axis_index("zh"), lax.axis_index("y")
    here = {"y": y, "zh": z}
    rows = pl.ds((lax.axis_index("x") * 2 + lax.axis_index("zl")) * SUB, SUB)
    partners = (
        [{"zh": at("zh", o)} for o in Z_OFF] + [{"y": at("y", o)} for o in Y_OFF] + [sibling()]
    )
    barrier = pltpu.get_barrier_semaphore()
    for d in partners:
        pl.semaphore_signal(barrier, inc=1, device_id=d, device_id_type=MESH_ID)
    meta[...] = jnp.zeros_like(meta)
    loads = [
        pltpu.make_async_copy(src, dst, local.at[i])
        for i, (src, dst) in enumerate(
            (
                (gate.at[0], raw.at[0]),
                (up.at[0], raw.at[1]),
                (down.at[0, rows], own_b),
                (col, lists.at[0]),
                (in_row, lists.at[1]),
                (out_row, lists.at[2]),
                (tok, tok_v),
                (cot, cot_v),
            )
        )
    ]
    for copy in loads:
        copy.start()
    for i in range(2):
        loads[i].wait()
    turned = [raw[i].astype(F32).T.astype(BF16) for i in range(2)]
    for i in range(2):
        raw[i] = turned[i]
    for i in range(2):
        own_a[i * SUB : (i + 1) * SUB] = raw[i, rows]
    loads[2].wait()
    a_in[c, y, z] = own_a[...]
    b_in[c, y, z] = own_b[...]

    @pl.loop(0, 8)
    def _(t):
        w[t] = jnp.zeros_like(w[t])
        dn[t] = jnp.zeros_like(dn[t])

    for copy in loads[3:6]:
        copy.wait()
    meta[0:3, 0:NB] = lists[...]
    across = jnp.broadcast_to(meta[0:1].astype(F32), (BLK, BLK))
    order = lax.broadcasted_iota(jnp.int32, (BLK, BLK), 0)
    meta[3:4] = jnp.min(jnp.where(across == across.T, order, NB), axis=0, keepdims=True)
    pl.semaphore_wait(barrier, len(partners))

    def lay(t):
        core = t >> 2
        for i in range(8):
            yy, zz = (t & 3) * 2 + i // 4, i % 4
            lanes = slice(i * BLK, (i + 1) * BLK)
            w[t, i * SUB : (i + 1) * SUB, lanes] = a_in[core, yy, zz, 0:SUB]
            w[t, BLK + i * SUB : BLK + (i + 1) * SUB, lanes] = a_in[core, yy, zz, SUB:]
            dn[t, i * SUB : (i + 1) * SUB, lanes] = b_in[core, yy, zz]

    def on_core(core):
        parts = []
        for n, (own, buf) in enumerate(((own_a, a_in), (own_b, b_in))):
            first = GATHER_FIRST[core][n]
            parts.append((first, own, buf.at[core], buf.at[1 - core], n))
        parts.sort(key=lambda p: p[0])

        def cross(axis, n, o, src, dst):
            i = n * 16 + (8 if axis == "zh" else 0) + o
            return send(src, dst, s_sem.at[i], r_sem.at[i], {axis: at(axis, o)})

        one, two, shared = {}, {}, []
        for first, own, buf, _, n in parts:
            one[n] = [cross(first, n, o, own, buf.at[y, z]) for o in OFF[first]]

        def share(axis, buf, o, n):
            part = line(buf, axis, at(axis, -o))
            i = n * 8 + o
            shared.append(send(part, part, s_sib.at[i], r_sib.at[i], sibling()))

        for first, _, buf, _, n in parts[::-1]:
            for copy in one[n]:
                copy.wait_recv()
            held = line(buf, OTHER[first], here[OTHER[first]])
            two[n] = [cross(OTHER[first], n, o, held, held) for o in OFF[OTHER[first]]]
            share(OTHER[first], buf, 0, n)
        (_, _, z_buf, _, zn), (_, _, y_buf, _, yn) = parts
        arrivals = list(zip(Y_OFF, two[yn]))[::-1]
        for o, copy in arrivals[:4]:
            copy.wait_recv()
            share("y", y_buf, o, yn)
        for o, copy in list(zip(Z_OFF, two[zn]))[::-1]:
            copy.wait_recv()
            share("zh", z_buf, o, zn)
        for o, copy in arrivals[4:]:
            copy.wait_recv()
            share("y", y_buf, o, yn)
        for copy in shared + one[0] + one[1] + two[0] + two[1]:
            copy.wait_send()

    def from_sibling(core):
        for n, buf in enumerate((a_in, b_in)):
            axis = OTHER[GATHER_FIRST[1 - core][n]]
            for o in (0, *OFF[axis]):
                part = line(buf.at[1 - core], axis, at(axis, -o))
                i = n * 8 + o
                pltpu.make_async_remote_copy(
                    src_ref=part,
                    dst_ref=part,
                    send_sem=s_sib.at[i],
                    recv_sem=r_sib.at[i],
                    device_id=sibling(),
                    device_id_type=MESH_ID,
                ).wait_recv()

    for core in range(2):
        pl.when(c == core)(lambda core=core: on_core(core))
    for copy in loads[6:]:
        copy.wait()

    @pl.loop(0, 4)
    def _(j):
        lay(c * 4 + j)

    for core in range(2):
        pl.when(c == core)(lambda core=core: from_sibling(core))

    @pl.loop(0, 4)
    def _(j):
        lay((1 - c) * 4 + j)


def gathered(*args):
    hbm = pl.BlockSpec(memory_space=pltpu.HBM)
    vmem = pl.BlockSpec(memory_space=pltpu.VMEM)
    return pl.pallas_call(
        gather_kernel,
        name="gather_blocks",
        out_shape=(
            jax.ShapeDtypeStruct((8, 256, 1024), BF16),
            jax.ShapeDtypeStruct((8, 128, 1024), BF16),
            jax.ShapeDtypeStruct((TOK, D), BF16),
            jax.ShapeDtypeStruct((TOK, D), BF16),
            jax.ShapeDtypeStruct((8, BLK), jnp.int32),
        ),
        in_specs=[hbm] * 8,
        out_specs=(vmem,) * 5,
        scratch_shapes=[
            pltpu.VMEM((2, 8, 4, 2 * SUB, BLK), BF16),
            pltpu.VMEM((2, 8, 4, SUB, BLK), BF16),
            pltpu.VMEM((2 * SUB, BLK), BF16),
            pltpu.VMEM((SUB, BLK), BF16),
            pltpu.VMEM((2, BLK, BLK), BF16),
            pltpu.VMEM((3, NB), jnp.int32),
            pltpu.SemaphoreType.DMA((32,)),
            pltpu.SemaphoreType.DMA((32,)),
            pltpu.SemaphoreType.DMA((16,)),
            pltpu.SemaphoreType.DMA((16,)),
            pltpu.SemaphoreType.DMA((8,)),
        ],
        compiler_params=pltpu.CompilerParams(
            collective_id=0, has_side_effects=True, vmem_limit_bytes=24 << 20
        ),
    )(*args)


def place_of(k):
    return ((k & 1) << 5) | (((k >> 1) & 7) << 2) | (k >> 4)


def dot_nt(a, b):
    return lax.dot_general(a, b, (((1,), (1,)), ((), ())), preferred_element_type=F32)


def dot(a, b):
    return jnp.dot(a, b, preferred_element_type=F32)


def compute_kernel(
    w, dn, tok, cot, meta, part, wa, wb, acc, g_s, u_s, h_s, table, pairs, sem
):
    load = pltpu.make_async_copy(meta, table, sem)
    load.start()
    load.wait()

    @pl.loop(0, 8, unroll=2)
    def _(t):
        acc[pl.ds(t * 4, 4)] = jnp.zeros((4, TOK, BLK), F32)
        rows_of = (lambda k: table[1, k]), (lambda k: table[2, k])
        g_s[t], u_s[t], h_s[t] = forward(t, tok, cot, *rows_of, w, dn)

    count = jnp.int32(0)
    for k in range(NB):
        first = table[3, k]
        pairs[count] = place_of(k) | (place_of(first) << 8)
        count = count + (first != k).astype(jnp.int32)
    group = lax.broadcasted_iota(jnp.int32, (TOK, BLK), 1) // SUB

    @pl.loop(0, count)
    def _(n):
        p, q = pairs[n] & 255, pairs[n] >> 8
        shift = ((q - p) * SUB) & (BLK - 1)
        for s in (g_s, u_s, h_s):
            moved = pltpu.roll(s[p >> 3], shift, axis=1)
            s[q >> 3] += jnp.where(group == (q & 7), moved, 0.0)

    @pl.loop(0, count)
    def _(n):
        p, q = pairs[n] & 255, pairs[n] >> 8
        shift = ((p - q) * SUB) & (BLK - 1)
        for s in (g_s, u_s, h_s):
            moved = pltpu.roll(s[q >> 3], shift, axis=1)
            s[p >> 3] = jnp.where(group == (p & 7), moved, s[p >> 3])

    @pl.loop(0, 8, unroll=2)
    def _(t):
        gate, up, hg = g_s[t], u_s[t], h_s[t]
        sig = jax.nn.sigmoid(gate)
        act = gate * sig
        hid = (act * up).T.astype(BF16)
        gg = hg * up * sig * (1.0 + gate * (1.0 - sig))
        ug = hg * act
        ggt, ugt = gg.T.astype(BF16), ug.T.astype(BF16)
        spread = dot(jnp.concatenate([gg.astype(BF16), ug.astype(BF16)], axis=1), w[t])
        for i in range(8):
            acc[table[1, flat(t, i)]] += spread[:, i * BLK : (i + 1) * BLK]
        core = t >> 2
        for j in range(4):
            rows = slice(32 * j, 32 * j + 32)
            ks = [flat(t, 2 * j), flat(t, 2 * j + 1)]
            left = jnp.concatenate([ggt[rows], ugt[rows]], axis=0)
            r = dot(left, jnp.concatenate([columns(tok, table[1, k]) for k in ks], axis=1))
            d = dot(hid[rows], jnp.concatenate([columns(cot, table[2, k]) for k in ks], axis=1))
            for n in range(2):
                i = 2 * j + n
                yy, zz = (t & 3) * 2 + i // 4, i % 4
                lanes = slice(n * BLK, (n + 1) * BLK)
                wa[core, yy, zz, 0:SUB] = r[n * SUB : (n + 1) * SUB, lanes]
                wa[core, yy, zz, SUB:] = r[32 + n * SUB : 32 + (n + 1) * SUB, lanes]
                wb[core, yy, zz] = d[n * SUB : (n + 1) * SUB, lanes]

    for m in range(8):
        for j in range(4):
            part[m, :, j * BLK : (j + 1) * BLK] = acc[4 * m + j].astype(BF16)


def computed(*args):
    vmem = pl.BlockSpec(memory_space=pltpu.VMEM)
    return pl.pallas_call(
        compute_kernel,
        name="block_grads",
        out_shape=(
            jax.ShapeDtypeStruct((8, TOK, 512), BF16),
            jax.ShapeDtypeStruct((2, 8, 4, 2 * SUB, BLK), F32),
            jax.ShapeDtypeStruct((2, 8, 4, SUB, BLK), F32),
        ),
        in_specs=[vmem] * 5,
        out_specs=(vmem,) * 3,
        scratch_shapes=[
            pltpu.VMEM((32, TOK, BLK), F32),
            pltpu.VMEM((8, TOK, BLK), F32),
            pltpu.VMEM((8, TOK, BLK), F32),
            pltpu.VMEM((8, TOK, BLK), F32),
            pltpu.SMEM((8, BLK), jnp.int32),
            pltpu.SMEM((BLK,), jnp.int32),
            pltpu.SemaphoreType.DMA,
        ],
        compiler_params=pltpu.CompilerParams(vmem_limit_bytes=24 << 20),
    )(*args)


def reduce_kernel(
    part, wa, wb, ig_in, fin,
    mid, sib_a, sib_b, sum_a, sum_b, ya, yb, za, zb, y2a, y2b, z2a, z2b,
    in_y2a, in_y2b, in_z2a, in_z2b,
    s_sem, r_sem, s_sib, r_sib, s_mp, r_mp, s_fin, r_fin,
):
    c, z, y = lax.axis_index("c"), lax.axis_index("zh"), lax.axis_index("y")
    x, zl = lax.axis_index("x"), lax.axis_index("zl")
    here = {"y": y, "zh": z}
    m = x * 2 + zl
    enter(
        [{"zh": at("zh", o)} for o in Z_OFF]
        + [{"y": at("y", o)} for o in Y_OFF]
        + [sibling()]
        + [mp_peer(o) for o in MP_OFF]
    )
    w, sib, acc = (wa, wb), (sib_a, sib_b), (sum_a, sum_b)
    in1 = {"y": (ya, yb), "zh": (za, zb)}
    sum2 = {"y": (y2a, y2b), "zh": (z2a, z2b)}
    in2 = {"y": (in_y2a, in_y2b), "zh": (in_z2a, in_z2b)}
    place = (pl.ds(0, 2 * SUB), pl.ds(2 * SUB, SUB))

    def on_core(core):
        mine = sorted((REDUCE_FIRST[core][n], n) for n in range(2))
        theirs = sorted((REDUCE_FIRST[1 - core][n], n) for n in range(2))
        sent, given = [], {}

        def sib_copy(n, axis, o, owner):
            i = n * 8 + o
            q = at(axis, o)
            return pltpu.make_async_remote_copy(
                src_ref=line(w[n].at[owner], axis, q),
                dst_ref=line(sib[n], axis, q),
                send_sem=s_sib.at[i],
                recv_sem=r_sib.at[i],
                device_id=sibling(),
                device_id_type=MESH_ID,
            )

        for axis, n in theirs:
            for o in (*OFF[axis], 0):
                copy = sib_copy(n, axis, o, 1 - core)
                copy.start()
                sent.append(copy)
        exch = []
        for h in range(2):
            for i, off in enumerate(X_OFF):
                q = at("x", off)
                k = h * 3 + i
                chunk = q * 2 + (1 - zl if h == 0 else zl)
                exch.append(send(part.at[chunk], ig_in.at[k], s_mp.at[k], r_mp.at[k], {"x": q}))
        for axis, n in mine:
            given[n] = []
            for o in (*OFF[axis], 0):
                sib_copy(n, axis, o, core).wait_recv()
                q = at(axis, o)
                if axis == "y":
                    acc[n][q] = (w[n][core, q] + sib[n][q]).astype(BF16)
                else:
                    acc[n][:, q] = (w[n][core, :, q] + sib[n][:, q]).astype(BF16)
                if o:
                    i = n * 32 + (8 if axis == "zh" else 0) + o
                    given[n].append(
                        send(
                            line(acc[n], axis, q), in1[axis][n].at[o],
                            s_sem.at[i], r_sem.at[i], {axis: q},
                        )
                    )
        second = {}
        for axis, n in mine[::-1]:
            q = here[axis]
            total = (acc[n][q] if axis == "y" else acc[n][:, q]).astype(F32)
            for o, copy in zip(OFF[axis], given[n]):
                copy.wait_recv()
                total += in1[axis][n][o].astype(F32)
            last_axis = OTHER[axis]
            sum2[last_axis][n][...] = total.astype(BF16)
            second[n] = []
            for o in OFF[last_axis]:
                i = n * 32 + 16 + (8 if last_axis == "zh" else 0) + o
                q = at(last_axis, o)
                second[n].append(
                    send(
                        sum2[last_axis][n].at[q], in2[last_axis][n].at[o],
                        s_sem.at[i], r_sem.at[i], {last_axis: q},
                    )
                )
        total = part[x * 2 + 1 - zl].astype(F32)
        for i in range(3):
            exch[i].wait_recv()
            total += ig_in[i].astype(F32)
        mid[...] = total.astype(BF16)
        exch.append(send(mid, ig_in.at[6], s_mp.at[6], r_mp.at[6], {"zl": 1 - zl}))
        for axis, n in mine[::-1]:
            last_axis = OTHER[axis]
            total = sum2[last_axis][n][here[last_axis]].astype(F32)
            for o, copy in zip(OFF[last_axis], second[n]):
                copy.wait_recv()
                total += in2[last_axis][n][o].astype(F32)
            fin[m, place[n]] = total.astype(fin.dtype)
        last = [
            send(fin.at[m], fin.at[m], s_fin.at[i], r_fin.at[i], mp_peer(off))
            for i, off in enumerate(MP_OFF)
        ]
        for copy in exch[3:] + last:
            copy.wait_recv()
        for copy in sent + exch + given[0] + given[1] + second[0] + second[1] + last:
            copy.wait_send()

    for core in range(2):
        pl.when(c == core)(lambda core=core: on_core(core))


def reduced(part, wa, wb):
    vmem = pl.BlockSpec(memory_space=pltpu.VMEM)

    def pair(*lead, kind=BF16):
        return [pltpu.VMEM((*lead, 2 * SUB, BLK), kind), pltpu.VMEM((*lead, SUB, BLK), kind)]

    return pl.pallas_call(
        reduce_kernel,
        name="sum_grads",
        out_shape=(
            jax.ShapeDtypeStruct((7, TOK, 512), BF16),
            jax.ShapeDtypeStruct((8, 3 * SUB, BLK), BF16),
        ),
        in_specs=[vmem] * 3,
        out_specs=(vmem,) * 2,
        scratch_shapes=[
            pltpu.VMEM((TOK, 512), BF16),
            *pair(8, 4, kind=F32),
            *pair(8, 4),
            *pair(8, 4),
            *pair(4, 8),
            *pair(8),
            *pair(4),
            *pair(8),
            *pair(4),
            pltpu.SemaphoreType.DMA((64,)),
            pltpu.SemaphoreType.DMA((64,)),
            pltpu.SemaphoreType.DMA((16,)),
            pltpu.SemaphoreType.DMA((16,)),
            pltpu.SemaphoreType.DMA((7,)),
            pltpu.SemaphoreType.DMA((7,)),
            pltpu.SemaphoreType.DMA((7,)),
            pltpu.SemaphoreType.DMA((7,)),
        ],
        compiler_params=pltpu.CompilerParams(
            collective_id=1, has_side_effects=True, vmem_limit_bytes=32 << 20
        ),
    )(part, wa, wb)


def finish_kernel(part, ig_in, fin, ig_out, g_out, u_out, d_out):
    total = part[lax.axis_index("x") * 2 + lax.axis_index("zl")].astype(F32)
    for i in range(3, 7):
        total += ig_in[i].astype(F32)
    ig_out[...] = total.astype(BF16)
    scale = 9216**-0.5
    g_out[0] = fin[:, 0:SUB].astype(F32).reshape(BLK, BLK).T * scale
    u_out[0] = fin[:, SUB : 2 * SUB].astype(F32).reshape(BLK, BLK).T * scale
    d_out[0] = fin[:, 2 * SUB :].astype(F32).reshape(BLK, BLK) * scale


def finished(part, ig_in, fin):
    vmem = pl.BlockSpec(memory_space=pltpu.VMEM)
    grad = jax.ShapeDtypeStruct((1, BLK, BLK), F32)
    return pl.pallas_call(
        finish_kernel,
        name="write_grads",
        out_shape=(jax.ShapeDtypeStruct((TOK, 512), BF16), grad, grad, grad),
        in_specs=[vmem] * 3,
        out_specs=(vmem,) * 4,
        compiler_params=pltpu.CompilerParams(vmem_limit_bytes=16 << 20),
    )(part, ig_in, fin)


def on_device(tokens, cotangent, gate, up, down, col_block, in_row, out_row):
    args = (gate, up, down, tokens, cotangent, col_block, in_row, out_row)
    tiles = gathered(*(pltpu.with_memory_space_constraint(a, pltpu.HBM) for a in args))
    part, wa, wb = computed(*tiles)
    return finished(part, *reduced(part, wa, wb))


def solution(mesh):
    fine = Mesh(mesh.devices.reshape(4, 8, 2, 4, 2), AXES)
    dp, mp = ("zh", "y", "c"), ("x", "zl")
    return jax.shard_map(
        on_device,
        mesh=fine,
        in_specs=(P(dp, None), P(dp, None), P(dp), P(dp), P(dp), P(), P(), P()),
        out_specs=(P(dp, mp), P(dp), P(dp), P(dp)),
        check_vma=False,
    )
```

```python
import jax
import jax.numpy as jnp
from jax import lax
from jax.experimental import pallas as pl
from jax.experimental.pallas import tpu as pltpu
from jax.sharding import Mesh
from jax.sharding import PartitionSpec as P

AXES = ("zh", "y", "c", "x", "zl")
SIZE = {"zh": 4, "y": 8, "c": 2, "x": 4, "zl": 2}
BLK = 128
TOK = 144
D = 4096
NB = 64
SUB = 16
MESH_ID = pl.DeviceIdType.MESH
F32, BF16 = jnp.float32, jnp.bfloat16
Y_OFF = (4, 3, 5, 2, 6, 1, 7)
Z_OFF = (2, 1, 3)
X_OFF = (2, 1, 3)
MP_OFF = ((2, 0), (2, 1), (1, 0), (3, 0), (1, 1), (3, 1), (0, 1))


def at(axis, offset):
    return lax.rem(lax.axis_index(axis) + (SIZE[axis] + offset), SIZE[axis])


def sibling():
    return {"c": 1 - lax.axis_index("c")}


def mp_peer(off):
    return {"x": at("x", off[0]), "zl": at("zl", off[1])}


def enter(devices):
    barrier = pltpu.get_barrier_semaphore()
    for d in devices:
        pl.semaphore_signal(barrier, inc=1, device_id=d, device_id_type=MESH_ID)
    pl.semaphore_wait(barrier, len(devices))


def send(src, dst, s, r, device):
    copy = pltpu.make_async_remote_copy(
        src_ref=src, dst_ref=dst, send_sem=s, recv_sem=r, device_id=device, device_id_type=MESH_ID
    )
    copy.start()
    return copy


OFF = {"y": Y_OFF, "zh": Z_OFF}
OTHER = {"y": "zh", "zh": "y"}
GATHER_FIRST = (("zh", "y"), ("y", "zh"))
REDUCE_FIRST = (("y", "zh"), ("zh", "y"))


def line(ref, axis, q):
    return ref.at[q] if axis == "y" else ref.at[pl.ds(0, SIZE["y"]), q]


def flat(t, i):
    return (i % 4) * 16 + (((t & 3) * 2 + i // 4) * 2) + (t >> 2)


def columns(ref, row):
    return ref[:, pl.ds(pl.multiple_of(row * BLK, BLK), BLK)]


def forward(t, tok, cot, in_row, out_row, w, dn):
    ks = [flat(t, i) for i in range(8)]
    gu = dot_nt(jnp.concatenate([columns(tok, in_row(k)) for k in ks], axis=1), w[t])
    hg = dot_nt(jnp.concatenate([columns(cot, out_row(k)) for k in ks], axis=1), dn[t])
    return gu[:, :BLK], gu[:, BLK:], hg


def gather_kernel(
    gate, up, down, tok, cot, col, in_row, out_row,
    w, dn, tok_v, cot_v, meta,
    a_in, b_in, own_a, own_b, raw, lists, s_sem, r_sem, s_sib, r_sib, local,
):
    c, z, y = lax.axis_index("c"), lax.axis_index("zh"), lax.axis_index("y")
    here = {"y": y, "zh": z}
    rows = pl.ds((lax.axis_index("x") * 2 + lax.axis_index("zl")) * SUB, SUB)
    partners = (
        [{"zh": at("zh", o)} for o in Z_OFF] + [{"y": at("y", o)} for o in Y_OFF] + [sibling()]
    )
    barrier = pltpu.get_barrier_semaphore()
    for d in partners:
        pl.semaphore_signal(barrier, inc=1, device_id=d, device_id_type=MESH_ID)
    meta[...] = jnp.zeros_like(meta)
    loads = [
        pltpu.make_async_copy(src, dst, local.at[i])
        for i, (src, dst) in enumerate(
            (
                (gate.at[0], raw.at[0]),
                (up.at[0], raw.at[1]),
                (down.at[0, rows], own_b),
                (col, lists.at[0]),
                (in_row, lists.at[1]),
                (out_row, lists.at[2]),
                (tok, tok_v),
                (cot, cot_v),
            )
        )
    ]
    for copy in loads:
        copy.start()
    for i in range(2):
        loads[i].wait()
    turned = [raw[i].astype(F32).T.astype(BF16) for i in range(2)]
    for i in range(2):
        raw[i] = turned[i]
    for i in range(2):
        own_a[i * SUB : (i + 1) * SUB] = raw[i, rows]
    loads[2].wait()
    a_in[c, y, z] = own_a[...]
    b_in[c, y, z] = own_b[...]

    pl.semaphore_wait(barrier, len(partners))

    def prepare():
        @pl.loop(0, 8)
        def _(t):
            w[t] = jnp.zeros_like(w[t])
            dn[t] = jnp.zeros_like(dn[t])

        for copy in loads[3:6]:
            copy.wait()
        meta[0:3, 0:NB] = lists[...]
        across = jnp.broadcast_to(meta[0:1].astype(F32), (BLK, BLK))
        order = lax.broadcasted_iota(jnp.int32, (BLK, BLK), 0)
        meta[3:4] = jnp.min(jnp.where(across == across.T, order, NB), axis=0, keepdims=True)

    def lay(t):
        core = t >> 2
        for i in range(8):
            yy, zz = (t & 3) * 2 + i // 4, i % 4
            lanes = slice(i * BLK, (i + 1) * BLK)
            w[t, i * SUB : (i + 1) * SUB, lanes] = a_in[core, yy, zz, 0:SUB]
            w[t, BLK + i * SUB : BLK + (i + 1) * SUB, lanes] = a_in[core, yy, zz, SUB:]
            dn[t, i * SUB : (i + 1) * SUB, lanes] = b_in[core, yy, zz]

    def on_core(core):
        parts = []
        for n, (own, buf) in enumerate(((own_a, a_in), (own_b, b_in))):
            first = GATHER_FIRST[core][n]
            parts.append((first, own, buf.at[core], buf.at[1 - core], n))
        parts.sort(key=lambda p: p[0])

        def cross(axis, n, o, src, dst):
            i = n * 16 + (8 if axis == "zh" else 0) + o
            return send(src, dst, s_sem.at[i], r_sem.at[i], {axis: at(axis, o)})

        one, two, shared = {}, {}, []
        for first, own, buf, _, n in parts:
            one[n] = [cross(first, n, o, own, buf.at[y, z]) for o in OFF[first]]

        prepare()

        def share(axis, buf, o, n):
            part = line(buf, axis, at(axis, -o))
            i = n * 8 + o
            shared.append(send(part, part, s_sib.at[i], r_sib.at[i], sibling()))

        for first, _, buf, _, n in parts[::-1]:
            for copy in one[n]:
                copy.wait_recv()
            held = line(buf, OTHER[first], here[OTHER[first]])
            two[n] = [cross(OTHER[first], n, o, held, held) for o in OFF[OTHER[first]]]
            share(OTHER[first], buf, 0, n)
        (_, _, z_buf, _, zn), (_, _, y_buf, _, yn) = parts
        arrivals = list(zip(Y_OFF, two[yn]))[::-1]
        for o, copy in arrivals[:4]:
            copy.wait_recv()
            share("y", y_buf, o, yn)
        for o, copy in list(zip(Z_OFF, two[zn]))[::-1]:
            copy.wait_recv()
            share("zh", z_buf, o, zn)
        for o, copy in arrivals[4:]:
            copy.wait_recv()
            share("y", y_buf, o, yn)
        for copy in shared + one[0] + one[1] + two[0] + two[1]:
            copy.wait_send()

    def from_sibling(core):
        for n, buf in enumerate((a_in, b_in)):
            axis = OTHER[GATHER_FIRST[1 - core][n]]
            for o in (0, *OFF[axis]):
                part = line(buf.at[1 - core], axis, at(axis, -o))
                i = n * 8 + o
                pltpu.make_async_remote_copy(
                    src_ref=part,
                    dst_ref=part,
                    send_sem=s_sib.at[i],
                    recv_sem=r_sib.at[i],
                    device_id=sibling(),
                    device_id_type=MESH_ID,
                ).wait_recv()

    for core in range(2):
        pl.when(c == core)(lambda core=core: on_core(core))
    for copy in loads[6:]:
        copy.wait()

    @pl.loop(0, 4)
    def _(j):
        lay(c * 4 + j)

    for core in range(2):
        pl.when(c == core)(lambda core=core: from_sibling(core))

    @pl.loop(0, 4)
    def _(j):
        lay((1 - c) * 4 + j)


def gathered(*args):
    hbm = pl.BlockSpec(memory_space=pltpu.HBM)
    vmem = pl.BlockSpec(memory_space=pltpu.VMEM)
    return pl.pallas_call(
        gather_kernel,
        name="gather_blocks",
        out_shape=(
            jax.ShapeDtypeStruct((8, 256, 1024), BF16),
            jax.ShapeDtypeStruct((8, 128, 1024), BF16),
            jax.ShapeDtypeStruct((TOK, D), BF16),
            jax.ShapeDtypeStruct((TOK, D), BF16),
            jax.ShapeDtypeStruct((8, BLK), jnp.int32),
        ),
        in_specs=[hbm] * 8,
        out_specs=(vmem,) * 5,
        scratch_shapes=[
            pltpu.VMEM((2, 8, 4, 2 * SUB, BLK), BF16),
            pltpu.VMEM((2, 8, 4, SUB, BLK), BF16),
            pltpu.VMEM((2 * SUB, BLK), BF16),
            pltpu.VMEM((SUB, BLK), BF16),
            pltpu.VMEM((2, BLK, BLK), BF16),
            pltpu.VMEM((3, NB), jnp.int32),
            pltpu.SemaphoreType.DMA((32,)),
            pltpu.SemaphoreType.DMA((32,)),
            pltpu.SemaphoreType.DMA((16,)),
            pltpu.SemaphoreType.DMA((16,)),
            pltpu.SemaphoreType.DMA((8,)),
        ],
        compiler_params=pltpu.CompilerParams(
            collective_id=0, has_side_effects=True, vmem_limit_bytes=24 << 20
        ),
    )(*args)


def place_of(k):
    return ((k & 1) << 5) | (((k >> 1) & 7) << 2) | (k >> 4)


def dot_nt(a, b):
    return lax.dot_general(a, b, (((1,), (1,)), ((), ())), preferred_element_type=F32)


def dot(a, b):
    return jnp.dot(a, b, preferred_element_type=F32)


def compute_kernel(
    w, dn, tok, cot, meta, part, wa, wb, acc, g_s, u_s, h_s, table, pairs, sem
):
    load = pltpu.make_async_copy(meta, table, sem)
    load.start()
    load.wait()

    @pl.loop(0, 8, unroll=8)
    def _(t):
        acc[pl.ds(t * 4, 4)] = jnp.zeros((4, TOK, BLK), F32)
        rows_of = (lambda k: table[1, k]), (lambda k: table[2, k])
        g_s[t], u_s[t], h_s[t] = forward(t, tok, cot, *rows_of, w, dn)

    count = jnp.int32(0)
    for k in range(NB):
        first = table[3, k]
        pairs[count] = place_of(k) | (place_of(first) << 8)
        count = count + (first != k).astype(jnp.int32)
    group = lax.broadcasted_iota(jnp.int32, (TOK, BLK), 1) // SUB

    @pl.loop(0, count)
    def _(n):
        p, q = pairs[n] & 255, pairs[n] >> 8
        shift = ((q - p) * SUB) & (BLK - 1)
        for s in (g_s, u_s, h_s):
            moved = pltpu.roll(s[p >> 3], shift, axis=1)
            s[q >> 3] += jnp.where(group == (q & 7), moved, 0.0)

    @pl.loop(0, count)
    def _(n):
        p, q = pairs[n] & 255, pairs[n] >> 8
        shift = ((p - q) * SUB) & (BLK - 1)
        for s in (g_s, u_s, h_s):
            moved = pltpu.roll(s[q >> 3], shift, axis=1)
            s[p >> 3] = jnp.where(group == (p & 7), moved, s[p >> 3])

    @pl.loop(0, 8, unroll=8)
    def _(t):
        gate, up, hg = g_s[t], u_s[t], h_s[t]
        sig = jax.nn.sigmoid(gate)
        act = gate * sig
        hid = (act * up).T.astype(BF16)
        gg = hg * up * sig * (1.0 + gate * (1.0 - sig))
        ug = hg * act
        ggt, ugt = gg.T.astype(BF16), ug.T.astype(BF16)
        spread = dot(jnp.concatenate([gg.astype(BF16), ug.astype(BF16)], axis=1), w[t])
        for i in range(8):
            acc[table[1, flat(t, i)]] += spread[:, i * BLK : (i + 1) * BLK]
        core = t >> 2
        for j in range(4):
            rows = slice(32 * j, 32 * j + 32)
            ks = [flat(t, 2 * j), flat(t, 2 * j + 1)]
            left = jnp.concatenate([ggt[rows], ugt[rows]], axis=0)
            r = dot(left, jnp.concatenate([columns(tok, table[1, k]) for k in ks], axis=1))
            d = dot(hid[rows], jnp.concatenate([columns(cot, table[2, k]) for k in ks], axis=1))
            for n in range(2):
                i = 2 * j + n
                yy, zz = (t & 3) * 2 + i // 4, i % 4
                lanes = slice(n * BLK, (n + 1) * BLK)
                wa[core, yy, zz, 0:SUB] = r[n * SUB : (n + 1) * SUB, lanes].astype(BF16)
                wa[core, yy, zz, SUB:] = r[32 + n * SUB : 48 + n * SUB, lanes].astype(BF16)
                wb[core, yy, zz] = d[n * SUB : (n + 1) * SUB, lanes].astype(BF16)

    for m in range(8):
        for j in range(4):
            part[m, :, j * BLK : (j + 1) * BLK] = acc[4 * m + j].astype(BF16)


def computed(*args):
    vmem = pl.BlockSpec(memory_space=pltpu.VMEM)
    return pl.pallas_call(
        compute_kernel,
        name="block_grads",
        out_shape=(
            jax.ShapeDtypeStruct((8, TOK, 512), BF16),
            jax.ShapeDtypeStruct((2, 8, 4, 2 * SUB, BLK), BF16),
            jax.ShapeDtypeStruct((2, 8, 4, SUB, BLK), BF16),
        ),
        in_specs=[vmem] * 5,
        out_specs=(vmem,) * 3,
        scratch_shapes=[
            pltpu.VMEM((32, TOK, BLK), F32),
            pltpu.VMEM((8, TOK, BLK), F32),
            pltpu.VMEM((8, TOK, BLK), F32),
            pltpu.VMEM((8, TOK, BLK), F32),
            pltpu.SMEM((8, BLK), jnp.int32),
            pltpu.SMEM((BLK,), jnp.int32),
            pltpu.SemaphoreType.DMA,
        ],
        compiler_params=pltpu.CompilerParams(vmem_limit_bytes=24 << 20),
    )(*args)


def add(a, b):
    return (a.astype(F32) + b.astype(F32)).astype(BF16)


def reduce_kernel(
    part, wa, wb, ig_in, fin,
    mid, sib_a, sib_b, sum_a, sum_b, ya, yb, za, zb, y2a, y2b, z2a, z2b,
    in_y2a, in_y2b, in_z2a, in_z2b,
    s_sem, r_sem, s_sib, r_sib, s_mp, r_mp, s_fin, r_fin,
):
    c, z, y = lax.axis_index("c"), lax.axis_index("zh"), lax.axis_index("y")
    x, zl = lax.axis_index("x"), lax.axis_index("zl")
    here = {"y": y, "zh": z}
    m = x * 2 + zl
    enter(
        [{"zh": at("zh", o)} for o in Z_OFF]
        + [{"y": at("y", o)} for o in Y_OFF]
        + [sibling()]
        + [mp_peer(o) for o in MP_OFF]
    )
    w, sib, acc = (wa, wb), (sib_a, sib_b), (sum_a, sum_b)
    in1 = {"y": (ya, yb), "zh": (za, zb)}
    sum2 = {"y": (y2a, y2b), "zh": (z2a, z2b)}
    in2 = {"y": (in_y2a, in_y2b), "zh": (in_z2a, in_z2b)}
    place = (pl.ds(0, 2 * SUB), pl.ds(2 * SUB, SUB))

    def on_core(core):
        mine = sorted((REDUCE_FIRST[core][n], n) for n in range(2))
        theirs = sorted((REDUCE_FIRST[1 - core][n], n) for n in range(2))
        sent, given = [], {}

        def sib_copy(n, axis, o, owner):
            i = n * 8 + o
            q = at(axis, o)
            return pltpu.make_async_remote_copy(
                src_ref=line(w[n].at[owner], axis, q),
                dst_ref=line(sib[n], axis, q),
                send_sem=s_sib.at[i],
                recv_sem=r_sib.at[i],
                device_id=sibling(),
                device_id_type=MESH_ID,
            )

        for axis, n in theirs:
            for o in (*OFF[axis], 0):
                copy = sib_copy(n, axis, o, 1 - core)
                copy.start()
                sent.append(copy)
        exch = []
        for h in range(2):
            for i, off in enumerate(X_OFF):
                q = at("x", off)
                k = h * 3 + i
                chunk = q * 2 + (1 - zl if h == 0 else zl)
                exch.append(send(part.at[chunk], ig_in.at[k], s_mp.at[k], r_mp.at[k], {"x": q}))
        for axis, n in mine:
            given[n] = []
            for o in (*OFF[axis], 0):
                sib_copy(n, axis, o, core).wait_recv()
                q = at(axis, o)
                if axis == "y":
                    acc[n][q] = add(w[n][core, q], sib[n][q])
                else:
                    acc[n][:, q] = add(w[n][core, :, q], sib[n][:, q])
                if o:
                    i = n * 32 + (8 if axis == "zh" else 0) + o
                    given[n].append(
                        send(
                            line(acc[n], axis, q), in1[axis][n].at[o],
                            s_sem.at[i], r_sem.at[i], {axis: q},
                        )
                    )
        second = {}
        for axis, n in mine[::-1]:
            q = here[axis]
            total = (acc[n][q] if axis == "y" else acc[n][:, q]).astype(F32)
            for o, copy in zip(OFF[axis], given[n]):
                copy.wait_recv()
                total += in1[axis][n][o].astype(F32)
            last_axis = OTHER[axis]
            sum2[last_axis][n][...] = total.astype(BF16)
            second[n] = []
            for o in OFF[last_axis]:
                i = n * 32 + 16 + (8 if last_axis == "zh" else 0) + o
                q = at(last_axis, o)
                second[n].append(
                    send(
                        sum2[last_axis][n].at[q], in2[last_axis][n].at[o],
                        s_sem.at[i], r_sem.at[i], {last_axis: q},
                    )
                )
        total = part[x * 2 + 1 - zl].astype(F32)
        for i in range(3):
            exch[i].wait_recv()
            total += ig_in[i].astype(F32)
        mid[...] = total.astype(BF16)
        exch.append(send(mid, ig_in.at[6], s_mp.at[6], r_mp.at[6], {"zl": 1 - zl}))
        for axis, n in mine[::-1]:
            last_axis = OTHER[axis]
            total = sum2[last_axis][n][here[last_axis]].astype(F32)
            for o, copy in zip(OFF[last_axis], second[n]):
                copy.wait_recv()
                total += in2[last_axis][n][o].astype(F32)
            fin[m, place[n]] = total.astype(fin.dtype)
        last = [
            send(fin.at[m], fin.at[m], s_fin.at[i], r_fin.at[i], mp_peer(off))
            for i, off in enumerate(MP_OFF)
        ]
        for copy in exch[3:] + last:
            copy.wait_recv()
        for copy in sent + exch + given[0] + given[1] + second[0] + second[1] + last:
            copy.wait_send()

    for core in range(2):
        pl.when(c == core)(lambda core=core: on_core(core))


def reduced(part, wa, wb):
    vmem = pl.BlockSpec(memory_space=pltpu.VMEM)

    def pair(*lead):
        return [pltpu.VMEM((*lead, 2 * SUB, BLK), BF16), pltpu.VMEM((*lead, SUB, BLK), BF16)]

    return pl.pallas_call(
        reduce_kernel,
        name="sum_grads",
        out_shape=(
            jax.ShapeDtypeStruct((7, TOK, 512), BF16),
            jax.ShapeDtypeStruct((8, 3 * SUB, BLK), BF16),
        ),
        in_specs=[vmem] * 3,
        out_specs=(vmem,) * 2,
        scratch_shapes=[
            pltpu.VMEM((TOK, 512), BF16),
            *pair(8, 4),
            *pair(8, 4),
            *pair(8, 4),
            *pair(4, 8),
            *pair(8),
            *pair(4),
            *pair(8),
            *pair(4),
            pltpu.SemaphoreType.DMA((64,)),
            pltpu.SemaphoreType.DMA((64,)),
            pltpu.SemaphoreType.DMA((16,)),
            pltpu.SemaphoreType.DMA((16,)),
            pltpu.SemaphoreType.DMA((7,)),
            pltpu.SemaphoreType.DMA((7,)),
            pltpu.SemaphoreType.DMA((7,)),
            pltpu.SemaphoreType.DMA((7,)),
        ],
        compiler_params=pltpu.CompilerParams(
            collective_id=1, has_side_effects=True, vmem_limit_bytes=32 << 20
        ),
    )(part, wa, wb)


def finish_kernel(part, ig_in, fin, ig_out, g_out, u_out, d_out):
    total = part[lax.axis_index("x") * 2 + lax.axis_index("zl")].astype(F32)
    for i in range(3, 7):
        total += ig_in[i].astype(F32)
    ig_out[...] = total.astype(BF16)
    scale = 9216**-0.5
    g_out[0] = fin[:, 0:SUB].astype(F32).reshape(BLK, BLK).T * scale
    u_out[0] = fin[:, SUB : 2 * SUB].astype(F32).reshape(BLK, BLK).T * scale
    d_out[0] = fin[:, 2 * SUB :].astype(F32).reshape(BLK, BLK) * scale


def finished(part, ig_in, fin):
    vmem = pl.BlockSpec(memory_space=pltpu.VMEM)
    grad = jax.ShapeDtypeStruct((1, BLK, BLK), F32)
    return pl.pallas_call(
        finish_kernel,
        name="write_grads",
        out_shape=(jax.ShapeDtypeStruct((TOK, 512), BF16), grad, grad, grad),
        in_specs=[vmem] * 3,
        out_specs=(vmem,) * 4,
        compiler_params=pltpu.CompilerParams(vmem_limit_bytes=16 << 20),
    )(part, ig_in, fin)


def on_device(tokens, cotangent, gate, up, down, col_block, in_row, out_row):
    args = (gate, up, down, tokens, cotangent, col_block, in_row, out_row)
    tiles = gathered(*(pltpu.with_memory_space_constraint(a, pltpu.HBM) for a in args))
    part, wa, wb = computed(*tiles)
    return finished(part, *reduced(part, wa, wb))


def solution(mesh):
    fine = Mesh(mesh.devices.reshape(4, 8, 2, 4, 2), AXES)
    dp, mp = ("zh", "y", "c"), ("x", "zl")
    return jax.shard_map(
        on_device,
        mesh=fine,
        in_specs=(P(dp, None), P(dp, None), P(dp), P(dp), P(dp), P(), P(), P()),
        out_specs=(P(dp, mp), P(dp), P(dp), P(dp)),
        check_vma=False,
    )
```

```python
import jax
import jax.numpy as jnp
from jax import lax
from jax.experimental import pallas as pl
from jax.experimental.pallas import tpu as pltpu
from jax.sharding import Mesh
from jax.sharding import PartitionSpec as P

AXES = ("zh", "y", "c", "x", "zl")
SIZE = {"zh": 4, "y": 8, "c": 2, "x": 4, "zl": 2}
BLK = 128
TOK = 144
D = 4096
NB = 64
SUB = 16
MESH_ID = pl.DeviceIdType.MESH
F32, BF16 = jnp.float32, jnp.bfloat16
Y_OFF = (4, 3, 5, 2, 6, 1, 7)
Z_OFF = (2, 1, 3)
X_OFF = (2, 1, 3)
MP_OFF = ((2, 0), (2, 1), (1, 0), (3, 0), (1, 1), (3, 1), (0, 1))


def at(axis, offset):
    return lax.rem(lax.axis_index(axis) + (SIZE[axis] + offset), SIZE[axis])


def sibling():
    return {"c": 1 - lax.axis_index("c")}


def mp_peer(off):
    return {"x": at("x", off[0]), "zl": at("zl", off[1])}


def enter(devices):
    barrier = pltpu.get_barrier_semaphore()
    for d in devices:
        pl.semaphore_signal(barrier, inc=1, device_id=d, device_id_type=MESH_ID)
    pl.semaphore_wait(barrier, len(devices))


def send(src, dst, s, r, device):
    copy = pltpu.make_async_remote_copy(
        src_ref=src, dst_ref=dst, send_sem=s, recv_sem=r, device_id=device, device_id_type=MESH_ID
    )
    copy.start()
    return copy


OFF = {"y": Y_OFF, "zh": Z_OFF}
OTHER = {"y": "zh", "zh": "y"}
GATHER_FIRST = (("zh", "y"), ("y", "zh"))
REDUCE_FIRST = (("y", "zh"), ("zh", "y"))


def line(ref, axis, q):
    return ref.at[q] if axis == "y" else ref.at[pl.ds(0, SIZE["y"]), q]


def flat(t, i):
    return (i % 4) * 16 + (((t & 3) * 2 + i // 4) * 2) + (t >> 2)


def columns(ref, row):
    return ref[:, pl.ds(pl.multiple_of(row * BLK, BLK), BLK)]


def forward(t, tok, cot, in_row, out_row, w, dn):
    ks = [flat(t, i) for i in range(8)]
    gu = dot_nt(jnp.concatenate([columns(tok, in_row(k)) for k in ks], axis=1), w[t])
    hg = dot_nt(jnp.concatenate([columns(cot, out_row(k)) for k in ks], axis=1), dn[t])
    return gu[:, :BLK], gu[:, BLK:], hg


def gather_kernel(
    gate, up, down, tok, cot, col, in_row, out_row,
    w, dn, tok_v, cot_v, meta,
    a_in, b_in, own_a, own_b, raw, lists, s_sem, r_sem, s_sib, r_sib, local,
):
    c, z, y = lax.axis_index("c"), lax.axis_index("zh"), lax.axis_index("y")
    here = {"y": y, "zh": z}
    rows = pl.ds((lax.axis_index("x") * 2 + lax.axis_index("zl")) * SUB, SUB)
    partners = (
        [{"zh": at("zh", o)} for o in Z_OFF] + [{"y": at("y", o)} for o in Y_OFF] + [sibling()]
    )
    barrier = pltpu.get_barrier_semaphore()
    for d in partners:
        pl.semaphore_signal(barrier, inc=1, device_id=d, device_id_type=MESH_ID)
    meta[...] = jnp.zeros_like(meta)
    loads = [
        pltpu.make_async_copy(src, dst, local.at[i])
        for i, (src, dst) in enumerate(
            (
                (gate.at[0], raw.at[0]),
                (up.at[0], raw.at[1]),
                (down.at[0, rows], own_b),
                (col, lists.at[0]),
                (in_row, lists.at[1]),
                (out_row, lists.at[2]),
                (tok, tok_v),
                (cot, cot_v),
            )
        )
    ]
    for copy in loads:
        copy.start()
    for i in range(2):
        loads[i].wait()
    turned = [raw[i].astype(F32).T.astype(BF16) for i in range(2)]
    for i in range(2):
        raw[i] = turned[i]
    for i in range(2):
        own_a[i * SUB : (i + 1) * SUB] = raw[i, rows]
    loads[2].wait()
    a_in[c, y, z] = own_a[...]
    b_in[c, y, z] = own_b[...]

    pl.semaphore_wait(barrier, len(partners))

    def prepare():
        @pl.loop(0, 8)
        def _(t):
            w[t] = jnp.zeros_like(w[t])
            dn[t] = jnp.zeros_like(dn[t])

        for copy in loads[3:6]:
            copy.wait()
        meta[0:3, 0:NB] = lists[...]
        across = jnp.broadcast_to(meta[0:1].astype(F32), (BLK, BLK))
        order = lax.broadcasted_iota(jnp.int32, (BLK, BLK), 0)
        meta[3:4] = jnp.min(jnp.where(across == across.T, order, NB), axis=0, keepdims=True)

    def lay(t):
        core = t >> 2
        for i in range(8):
            yy, zz = (t & 3) * 2 + i // 4, i % 4
            lanes = slice(i * BLK, (i + 1) * BLK)
            w[t, i * SUB : (i + 1) * SUB, lanes] = a_in[core, yy, zz, 0:SUB]
            w[t, BLK + i * SUB : BLK + (i + 1) * SUB, lanes] = a_in[core, yy, zz, SUB:]
            dn[t, i * SUB : (i + 1) * SUB, lanes] = b_in[core, yy, zz]

    def on_core(core):
        parts = []
        for n, (own, buf) in enumerate(((own_a, a_in), (own_b, b_in))):
            first = GATHER_FIRST[core][n]
            parts.append((first, own, buf.at[core], buf.at[1 - core], n))
        parts.sort(key=lambda p: p[0])

        def cross(axis, n, o, src, dst):
            i = n * 16 + (8 if axis == "zh" else 0) + o
            return send(src, dst, s_sem.at[i], r_sem.at[i], {axis: at(axis, o)})

        one, early, two, shared = {}, {}, {}, []
        for first, own, buf, _, n in parts:
            one[n] = [cross(first, n, o, own, buf.at[y, z]) for o in OFF[first]]
        for first, own, buf, _, n in parts[::-1]:
            after = OTHER[first]
            early[n] = [cross(after, n, o, own, buf.at[y, z]) for o in OFF[after]]

        prepare()

        def share(axis, buf, o, n):
            part = line(buf, axis, at(axis, -o))
            i = n * 8 + o
            shared.append(send(part, part, s_sib.at[i], r_sib.at[i], sibling()))

        for first, _, buf, _, n in parts[::-1]:
            after = OTHER[first]
            for o, copy in zip(OFF[first], one[n]):
                copy.wait_recv()
                q = at(first, -o)
                piece = buf.at[q, z] if first == "y" else buf.at[y, q]
                for p in OFF[after]:
                    cross(after, n, p, piece, piece)
            share(after, buf, 0, n)
            two[n] = []
            for o in OFF[after]:
                i = n * 16 + (8 if after == "zh" else 0) + o
                whole = line(buf, after, at(after, -o))
                two[n].append(
                    pltpu.make_async_remote_copy(
                        src_ref=whole,
                        dst_ref=whole,
                        send_sem=s_sem.at[i],
                        recv_sem=r_sem.at[i],
                        device_id={after: at(after, o)},
                        device_id_type=MESH_ID,
                    )
                )
        (_, _, z_buf, _, zn), (_, _, y_buf, _, yn) = parts
        arrivals = list(zip(Y_OFF, two[yn]))[::-1]
        for o, copy in arrivals[:4]:
            copy.wait_recv()
            share("y", y_buf, o, yn)
        for o, copy in list(zip(Z_OFF, two[zn]))[::-1]:
            copy.wait_recv()
            share("zh", z_buf, o, zn)
        for o, copy in arrivals[4:]:
            copy.wait_recv()
            share("y", y_buf, o, yn)
        for copy in shared + one[0] + one[1] + two[0] + two[1]:
            copy.wait_send()

    def from_sibling(core):
        for n, buf in enumerate((a_in, b_in)):
            axis = OTHER[GATHER_FIRST[1 - core][n]]
            for o in (0, *OFF[axis]):
                part = line(buf.at[1 - core], axis, at(axis, -o))
                i = n * 8 + o
                pltpu.make_async_remote_copy(
                    src_ref=part,
                    dst_ref=part,
                    send_sem=s_sib.at[i],
                    recv_sem=r_sib.at[i],
                    device_id=sibling(),
                    device_id_type=MESH_ID,
                ).wait_recv()

    for core in range(2):
        pl.when(c == core)(lambda core=core: on_core(core))
    for copy in loads[6:]:
        copy.wait()

    @pl.loop(0, 4)
    def _(j):
        lay(c * 4 + j)

    for core in range(2):
        pl.when(c == core)(lambda core=core: from_sibling(core))

    @pl.loop(0, 4)
    def _(j):
        lay((1 - c) * 4 + j)


def gathered(*args):
    hbm = pl.BlockSpec(memory_space=pltpu.HBM)
    vmem = pl.BlockSpec(memory_space=pltpu.VMEM)
    return pl.pallas_call(
        gather_kernel,
        name="gather_blocks",
        out_shape=(
            jax.ShapeDtypeStruct((8, 256, 1024), BF16),
            jax.ShapeDtypeStruct((8, 128, 1024), BF16),
            jax.ShapeDtypeStruct((TOK, D), BF16),
            jax.ShapeDtypeStruct((TOK, D), BF16),
            jax.ShapeDtypeStruct((8, BLK), jnp.int32),
        ),
        in_specs=[hbm] * 8,
        out_specs=(vmem,) * 5,
        scratch_shapes=[
            pltpu.VMEM((2, 8, 4, 2 * SUB, BLK), BF16),
            pltpu.VMEM((2, 8, 4, SUB, BLK), BF16),
            pltpu.VMEM((2 * SUB, BLK), BF16),
            pltpu.VMEM((SUB, BLK), BF16),
            pltpu.VMEM((2, BLK, BLK), BF16),
            pltpu.VMEM((3, NB), jnp.int32),
            pltpu.SemaphoreType.DMA((32,)),
            pltpu.SemaphoreType.DMA((32,)),
            pltpu.SemaphoreType.DMA((16,)),
            pltpu.SemaphoreType.DMA((16,)),
            pltpu.SemaphoreType.DMA((8,)),
        ],
        compiler_params=pltpu.CompilerParams(
            collective_id=0, has_side_effects=True, vmem_limit_bytes=24 << 20
        ),
    )(*args)


def place_of(k):
    return ((k & 1) << 5) | (((k >> 1) & 7) << 2) | (k >> 4)


def dot_nt(a, b):
    return lax.dot_general(a, b, (((1,), (1,)), ((), ())), preferred_element_type=F32)


def dot(a, b):
    return jnp.dot(a, b, preferred_element_type=F32)


def compute_kernel(
    w, dn, tok, cot, meta, part, wa, wb, acc, g_s, u_s, h_s, table, pairs, sem
):
    load = pltpu.make_async_copy(meta, table, sem)
    load.start()
    load.wait()

    @pl.loop(0, 8, unroll=8)
    def _(t):
        acc[pl.ds(t * 4, 4)] = jnp.zeros((4, TOK, BLK), F32)
        rows_of = (lambda k: table[1, k]), (lambda k: table[2, k])
        g_s[t], u_s[t], h_s[t] = forward(t, tok, cot, *rows_of, w, dn)

    count = jnp.int32(0)
    for k in range(NB):
        first = table[3, k]
        pairs[count] = place_of(k) | (place_of(first) << 8)
        count = count + (first != k).astype(jnp.int32)
    group = lax.broadcasted_iota(jnp.int32, (TOK, BLK), 1) // SUB

    @pl.loop(0, count)
    def _(n):
        p, q = pairs[n] & 255, pairs[n] >> 8
        shift = ((q - p) * SUB) & (BLK - 1)
        for s in (g_s, u_s, h_s):
            moved = pltpu.roll(s[p >> 3], shift, axis=1)
            s[q >> 3] += jnp.where(group == (q & 7), moved, 0.0)

    @pl.loop(0, count)
    def _(n):
        p, q = pairs[n] & 255, pairs[n] >> 8
        shift = ((p - q) * SUB) & (BLK - 1)
        for s in (g_s, u_s, h_s):
            moved = pltpu.roll(s[q >> 3], shift, axis=1)
            s[p >> 3] = jnp.where(group == (p & 7), moved, s[p >> 3])

    @pl.loop(0, 8, unroll=8)
    def _(t):
        gate, up, hg = g_s[t], u_s[t], h_s[t]
        sig = jax.nn.sigmoid(gate)
        act = gate * sig
        hid = (act * up).T.astype(BF16)
        gg = hg * up * sig * (1.0 + gate * (1.0 - sig))
        ug = hg * act
        ggt, ugt = gg.T.astype(BF16), ug.T.astype(BF16)
        spread = dot(jnp.concatenate([gg.astype(BF16), ug.astype(BF16)], axis=1), w[t])
        for i in range(8):
            acc[table[1, flat(t, i)]] += spread[:, i * BLK : (i + 1) * BLK]
        core = t >> 2
        for j in range(4):
            rows = slice(32 * j, 32 * j + 32)
            ks = [flat(t, 2 * j), flat(t, 2 * j + 1)]
            left = jnp.concatenate([ggt[rows], ugt[rows]], axis=0)
            r = dot(left, jnp.concatenate([columns(tok, table[1, k]) for k in ks], axis=1))
            d = dot(hid[rows], jnp.concatenate([columns(cot, table[2, k]) for k in ks], axis=1))
            for n in range(2):
                i = 2 * j + n
                yy, zz = (t & 3) * 2 + i // 4, i % 4
                lanes = slice(n * BLK, (n + 1) * BLK)
                wa[core, yy, zz, 0:SUB] = r[n * SUB : (n + 1) * SUB, lanes].astype(BF16)
                wa[core, yy, zz, SUB:] = r[32 + n * SUB : 48 + n * SUB, lanes].astype(BF16)
                wb[core, yy, zz] = d[n * SUB : (n + 1) * SUB, lanes].astype(BF16)

    for m in range(8):
        for j in range(4):
            part[m, :, j * BLK : (j + 1) * BLK] = acc[4 * m + j].astype(BF16)


def computed(*args):
    vmem = pl.BlockSpec(memory_space=pltpu.VMEM)
    return pl.pallas_call(
        compute_kernel,
        name="block_grads",
        out_shape=(
            jax.ShapeDtypeStruct((8, TOK, 512), BF16),
            jax.ShapeDtypeStruct((2, 8, 4, 2 * SUB, BLK), BF16),
            jax.ShapeDtypeStruct((2, 8, 4, SUB, BLK), BF16),
        ),
        in_specs=[vmem] * 5,
        out_specs=(vmem,) * 3,
        scratch_shapes=[
            pltpu.VMEM((32, TOK, BLK), F32),
            pltpu.VMEM((8, TOK, BLK), F32),
            pltpu.VMEM((8, TOK, BLK), F32),
            pltpu.VMEM((8, TOK, BLK), F32),
            pltpu.SMEM((8, BLK), jnp.int32),
            pltpu.SMEM((BLK,), jnp.int32),
            pltpu.SemaphoreType.DMA,
        ],
        compiler_params=pltpu.CompilerParams(vmem_limit_bytes=24 << 20),
    )(*args)


def add(a, b):
    return (a.astype(F32) + b.astype(F32)).astype(BF16)


def reduce_kernel(
    part, wa, wb, ig_in, fin,
    mid, sib_a, sib_b, sum_a, sum_b, ya, yb, za, zb, y2a, y2b, z2a, z2b,
    in_y2a, in_y2b, in_z2a, in_z2b,
    s_sem, r_sem, s_sib, r_sib, s_mp, r_mp, s_fin, r_fin,
):
    c, z, y = lax.axis_index("c"), lax.axis_index("zh"), lax.axis_index("y")
    x, zl = lax.axis_index("x"), lax.axis_index("zl")
    here = {"y": y, "zh": z}
    m = x * 2 + zl
    enter(
        [{"zh": at("zh", o)} for o in Z_OFF]
        + [{"y": at("y", o)} for o in Y_OFF]
        + [sibling()]
        + [mp_peer(o) for o in MP_OFF]
    )
    w, sib, acc = (wa, wb), (sib_a, sib_b), (sum_a, sum_b)
    in1 = {"y": (ya, yb), "zh": (za, zb)}
    sum2 = {"y": (y2a, y2b), "zh": (z2a, z2b)}
    in2 = {"y": (in_y2a, in_y2b), "zh": (in_z2a, in_z2b)}
    place = (pl.ds(0, 2 * SUB), pl.ds(2 * SUB, SUB))

    def on_core(core):
        mine = sorted((REDUCE_FIRST[core][n], n) for n in range(2))
        theirs = sorted((REDUCE_FIRST[1 - core][n], n) for n in range(2))
        sent, given = [], {}

        def sib_copy(n, axis, o, owner):
            i = n * 8 + o
            q = at(axis, o)
            return pltpu.make_async_remote_copy(
                src_ref=line(w[n].at[owner], axis, q),
                dst_ref=line(sib[n], axis, q),
                send_sem=s_sib.at[i],
                recv_sem=r_sib.at[i],
                device_id=sibling(),
                device_id_type=MESH_ID,
            )

        for axis, n in theirs:
            for o in (*OFF[axis], 0):
                copy = sib_copy(n, axis, o, 1 - core)
                copy.start()
                sent.append(copy)
        exch = []
        for h in range(2):
            for i, off in enumerate(X_OFF):
                q = at("x", off)
                k = h * 3 + i
                chunk = q * 2 + (1 - zl if h == 0 else zl)
                exch.append(send(part.at[chunk], ig_in.at[k], s_mp.at[k], r_mp.at[k], {"x": q}))
        for axis, n in mine:
            given[n] = []
            for o in (*OFF[axis], 0):
                sib_copy(n, axis, o, core).wait_recv()
                q = at(axis, o)
                if axis == "y":
                    acc[n][q] = add(w[n][core, q], sib[n][q])
                else:
                    acc[n][:, q] = add(w[n][core, :, q], sib[n][:, q])
                if o:
                    i = n * 32 + (8 if axis == "zh" else 0) + o
                    given[n].append(
                        send(
                            line(acc[n], axis, q), in1[axis][n].at[o],
                            s_sem.at[i], r_sem.at[i], {axis: q},
                        )
                    )
        second = {}
        for axis, n in mine[::-1]:
            q = here[axis]
            total = (acc[n][q] if axis == "y" else acc[n][:, q]).astype(F32)
            for o, copy in zip(OFF[axis], given[n]):
                copy.wait_recv()
                total += in1[axis][n][o].astype(F32)
            last_axis = OTHER[axis]
            sum2[last_axis][n][...] = total.astype(BF16)
            second[n] = []
            for o in OFF[last_axis]:
                i = n * 32 + 16 + (8 if last_axis == "zh" else 0) + o
                q = at(last_axis, o)
                second[n].append(
                    send(
                        sum2[last_axis][n].at[q], in2[last_axis][n].at[o],
                        s_sem.at[i], r_sem.at[i], {last_axis: q},
                    )
                )
        total = part[x * 2 + 1 - zl].astype(F32)
        for i in range(3):
            exch[i].wait_recv()
            total += ig_in[i].astype(F32)
        mid[...] = total.astype(BF16)
        exch.append(send(mid, ig_in.at[6], s_mp.at[6], r_mp.at[6], {"zl": 1 - zl}))
        for axis, n in mine[::-1]:
            last_axis = OTHER[axis]
            total = sum2[last_axis][n][here[last_axis]].astype(F32)
            for o, copy in zip(OFF[last_axis], second[n]):
                copy.wait_recv()
                total += in2[last_axis][n][o].astype(F32)
            fin[m, place[n]] = total.astype(fin.dtype)
        last = [
            send(fin.at[m], fin.at[m], s_fin.at[i], r_fin.at[i], mp_peer(off))
            for i, off in enumerate(MP_OFF)
        ]
        for copy in exch[3:] + last:
            copy.wait_recv()
        for copy in sent + exch + given[0] + given[1] + second[0] + second[1] + last:
            copy.wait_send()

    for core in range(2):
        pl.when(c == core)(lambda core=core: on_core(core))


def reduced(part, wa, wb):
    vmem = pl.BlockSpec(memory_space=pltpu.VMEM)

    def pair(*lead):
        return [pltpu.VMEM((*lead, 2 * SUB, BLK), BF16), pltpu.VMEM((*lead, SUB, BLK), BF16)]

    return pl.pallas_call(
        reduce_kernel,
        name="sum_grads",
        out_shape=(
            jax.ShapeDtypeStruct((7, TOK, 512), BF16),
            jax.ShapeDtypeStruct((8, 3 * SUB, BLK), BF16),
        ),
        in_specs=[vmem] * 3,
        out_specs=(vmem,) * 2,
        scratch_shapes=[
            pltpu.VMEM((TOK, 512), BF16),
            *pair(8, 4),
            *pair(8, 4),
            *pair(8, 4),
            *pair(4, 8),
            *pair(8),
            *pair(4),
            *pair(8),
            *pair(4),
            pltpu.SemaphoreType.DMA((64,)),
            pltpu.SemaphoreType.DMA((64,)),
            pltpu.SemaphoreType.DMA((16,)),
            pltpu.SemaphoreType.DMA((16,)),
            pltpu.SemaphoreType.DMA((7,)),
            pltpu.SemaphoreType.DMA((7,)),
            pltpu.SemaphoreType.DMA((7,)),
            pltpu.SemaphoreType.DMA((7,)),
        ],
        compiler_params=pltpu.CompilerParams(
            collective_id=1, has_side_effects=True, vmem_limit_bytes=32 << 20
        ),
    )(part, wa, wb)


def finish_kernel(part, ig_in, fin, ig_out, g_out, u_out, d_out):
    total = part[lax.axis_index("x") * 2 + lax.axis_index("zl")].astype(F32)
    for i in range(3, 7):
        total += ig_in[i].astype(F32)
    ig_out[...] = total.astype(BF16)
    scale = 9216**-0.5
    g_out[0] = fin[:, 0:SUB].astype(F32).reshape(BLK, BLK).T * scale
    u_out[0] = fin[:, SUB : 2 * SUB].astype(F32).reshape(BLK, BLK).T * scale
    d_out[0] = fin[:, 2 * SUB :].astype(F32).reshape(BLK, BLK) * scale


def finished(part, ig_in, fin):
    vmem = pl.BlockSpec(memory_space=pltpu.VMEM)
    grad = jax.ShapeDtypeStruct((1, BLK, BLK), F32)
    return pl.pallas_call(
        finish_kernel,
        name="write_grads",
        out_shape=(jax.ShapeDtypeStruct((TOK, 512), BF16), grad, grad, grad),
        in_specs=[vmem] * 3,
        out_specs=(vmem,) * 4,
        compiler_params=pltpu.CompilerParams(vmem_limit_bytes=16 << 20),
    )(part, ig_in, fin)


def on_device(tokens, cotangent, gate, up, down, col_block, in_row, out_row):
    args = (gate, up, down, tokens, cotangent, col_block, in_row, out_row)
    tiles = gathered(*(pltpu.with_memory_space_constraint(a, pltpu.HBM) for a in args))
    part, wa, wb = computed(*tiles)
    return finished(part, *reduced(part, wa, wb))


def solution(mesh):
    fine = Mesh(mesh.devices.reshape(4, 8, 2, 4, 2), AXES)
    dp, mp = ("zh", "y", "c"), ("x", "zl")
    return jax.shard_map(
        on_device,
        mesh=fine,
        in_specs=(P(dp, None), P(dp, None), P(dp), P(dp), P(dp), P(), P(), P()),
        out_specs=(P(dp, mp), P(dp), P(dp), P(dp)),
        check_vma=False,
    )
```
